128 devices in a mesh: layer: 4 (over z_hi, core), row: 4 (over x), col: 8 (over y, z_lo).
Axes of the slice: x: 4, y: 4, z: 4 (z_hi: 2, z_lo: 2; z = z_hi * 2 + z_lo), core: 2. Of those that a mesh axis runs over, the one named last changes fastest.
Arguments:
- traces_rows: bfloat16 [64, 2048, 4096], P(None, 'row', ('layer', 'col')), may hold values from -6 to 6
- traces_cols: bfloat16 [64, 2048, 4096], P(None, 'col', ('layer', 'row')), may hold values from -6 to 6
- offsets_rows: int32 [2048], P('row'), may hold values from 0 to 16
- offsets_cols: int32 [2048], P('col'), may hold values from 0 to 16
- bins: int32 [8], replicated, may hold values from 1 to 511
Outputs:
- c3: float32 [8, 2, 2048, 2048], P('layer', None, 'row', 'col')
The draws below stay inside these ranges and needn't reach their ends.
Inputs may be any that keep to these rules, and one draw needn't show every extreme that they name: `bins`: bin indices, not necessarily distinct.
All inputs are finite; a program needn't handle non-finite values.
Results may differ from the reference program's by a relative error of at most 0.0054.
Values may be sent and summed in bfloat16 or wider, within the bound.
No kernel may reach another device: no remote copies, remote signals or barrier semaphores. Data moves between devices by JAX's collectives and lax.ppermute only.
A program may use at most 192 MiB of HBM per device.

```python
import math
import jax
import jax.numpy as jnp
from jax import lax

F = 8
NFFT = 1024
SAMPLES = 64
WINDOW = 48
K_AUX = 4096
NI = 2048
NJ = 2048


def with_ends(drawn, own_key, low, largest):
    spot = [jax.random.randint(jax.random.fold_in(own_key, axis), (), 0, length) for axis, length in enumerate(drawn.shape)]
    longest = drawn.shape.index(max(drawn.shape))
    beside = spot[:longest] + [(spot[longest] + 1) % drawn.shape[longest]] + spot[longest + 1:]
    return drawn.at[tuple(spot)].set(low).at[tuple(beside)].set(largest)


def block_scale(own_key, shape, cuts, smallest, top_value):
    loudness = 1.0
    for position, shards_of in cuts:
        draws = jax.random.uniform(jax.random.fold_in(jax.random.fold_in(own_key, 6), position), (shards_of,), jnp.float32, smallest / len(cuts), top_value / len(cuts))
        loudness = loudness * jnp.repeat(jnp.exp(draws), shape[position] // shards_of).reshape((-1,) + (1,) * (len(shape) - 1 - position))
    return loudness


def gaussian(stream_key, extent, width, most, cuts=(), kind=jnp.bfloat16):
    gain = block_scale(stream_key, extent, cuts, -0.22, 0.18) if cuts else 1.0
    entries = jax.random.normal(stream_key, extent, jnp.float32) * width * gain
    return jnp.minimum(jnp.maximum(entries, -most), most).astype(kind)


def setup_inputs(seed: int = 0) -> dict:
    key_of = jax.random.split(jax.random.key(seed), 6)
    traces_rows = gaussian(key_of[0], (SAMPLES, NI, K_AUX), 1.0, 6.0, ((1, 4), (2, 32)))
    traces_cols = gaussian(key_of[1], (SAMPLES, NJ, K_AUX), 1.0, 6.0, ((1, 8), (2, 16)))
    offsets_rows = with_ends(jax.random.randint(key_of[2], (NI,), 0, SAMPLES - WINDOW + 1), jax.random.fold_in(key_of[2], 1), 0, SAMPLES - WINDOW).astype(jnp.int32)
    offsets_cols = with_ends(jax.random.randint(key_of[3], (NJ,), 0, SAMPLES - WINDOW + 1), jax.random.fold_in(key_of[3], 1), 0, SAMPLES - WINDOW).astype(jnp.int32)
    bins = with_ends(jax.random.randint(key_of[4], (F,), 1, NFFT // 2), jax.random.fold_in(key_of[4], 1), 1, (NFFT // 2) - 1).astype(jnp.int32)
    return {"traces_rows": traces_rows, "traces_cols": traces_cols, "offsets_rows": offsets_rows, "offsets_cols": offsets_cols, "bins": bins}


def make_basis(offsets, bins):
    tick = jnp.arange(SAMPLES, dtype=jnp.int32)
    lag = tick[:, None] - offsets[None, :].astype(jnp.int32)
    inside = (lag >= 0) & (lag < WINDOW)
    lagf = lag.astype(jnp.float32)
    taper = 0.5 - 0.5 * jnp.cos(2.0 * math.pi * (lagf + 0.5) / WINDOW)
    clipped = jnp.clip(lag, 0, WINDOW - 1)
    phase_int = (bins.astype(jnp.int32)[None, :, None] * clipped[:, None, :]) % NFFT
    angle = 2.0 * math.pi * phase_int.astype(jnp.float32) / NFFT
    weight = jnp.where(inside, taper, 0.0).astype(jnp.float32)[:, None, :]
    real = weight * jnp.cos(angle)
    imag = -weight * jnp.sin(angle)
    return jnp.stack([real, imag], axis=2).astype(jnp.bfloat16)


def spectra(traces, offsets, bins):
    count = traces.shape[1]
    block = min(256, count)
    pieces = []
    for first in range(0, count, block):
        part = traces[:, first:first + block, :].astype(jnp.float32)
        basis = make_basis(offsets[first:first + block], bins).astype(jnp.float32)
        pieces.append(jnp.einsum('tnk,tfpn->fnpk', part, basis).astype(jnp.bfloat16))
    return jnp.concatenate(pieces, axis=1)


def reference(traces_rows, traces_cols, offsets_rows, offsets_cols, bins):
    spec_rows = spectra(traces_rows, offsets_rows, bins)
    spec_cols = spectra(traces_cols, offsets_cols, bins)

    def one_bin(pair):
        left, right = pair
        real = left[:, 0, :]
        imag = left[:, 1, :]
        second = jnp.stack([imag, -real], axis=1)
        doubled = jnp.stack([left, second], axis=0).astype(jnp.float32)
        return jnp.einsum('cipk,jpk->cij', doubled, right.astype(jnp.float32))

    total = lax.map(one_bin, (spec_rows, spec_cols))
    return total * (1.0 / K_AUX)
```

```python
import functools
import math

import jax
import jax.numpy as jnp
from jax import lax
from jax.experimental import pallas as pl
from jax.experimental.pallas import tpu as pltpu
from jax.sharding import PartitionSpec as P

NFFT = 1024
SAMPLES = 64
WINDOW = 48
K_AUX = 4096
AXES = ("layer", "row", "col")
GROUP = 16
STEP = 64
BF16 = jnp.bfloat16
F32 = jnp.float32


def permutation(dest):
    pairs = []
    for layer in range(4):
        for row in range(4):
            for col in range(8):
                z, core = 2 * (layer // 2) + col % 2, layer % 2
                x, y, z, core2 = dest(row, col // 2, z, core)
                to = ((z // 2) * 2 + core2) * 32 + x * 8 + y * 2 + z % 2
                pairs.append(((layer * 4 + row) * 8 + col, to))
    return pairs


def near(core):
    return 3 if core else 1


def far(core):
    return 1 if core else 3


Y_A = permutation(lambda x, y, z, c: (x, y ^ near(c), z, c))
Y_B = permutation(lambda x, y, z, c: (x, y ^ far(c), z, c))
X_A = permutation(lambda x, y, z, c: (x ^ near(c), y, z, c))
X_B = permutation(lambda x, y, z, c: (x ^ far(c), y, z, c))
SLOTS = [
    permutation(lambda x, y, z, c: (x, y, z, 1 - c)),
    permutation(lambda x, y, z, c: (x, y, z ^ near(c), c)),
    permutation(lambda x, y, z, c: (x, y, z ^ far(c), 1 - c)),
    permutation(lambda x, y, z, c: (x, y, z ^ far(c), c)),
    permutation(lambda x, y, z, c: (x, y, z ^ near(c), 1 - c)),
    permutation(lambda x, y, z, c: (x, y, z ^ 2, c)),
    permutation(lambda x, y, z, c: (x, y, z ^ 2, 1 - c)),
]
HALVES = permutation(lambda x, y, z, c: (x, y, z ^ 1, c))


def send(value, pairs):
    return lax.ppermute(value, AXES, pairs)


def after(value, *others):
    return lax.optimization_barrier((value,) + others)[0]


def basis_table(bins):
    lag = jnp.arange(SAMPLES, dtype=jnp.int32)
    taper = 0.5 - 0.5 * jnp.cos(2.0 * math.pi * (lag.astype(F32) + 0.5) / WINDOW)
    clipped = jnp.clip(lag, 0, WINDOW - 1)
    phase = bins[:, None] * clipped[None, :] % NFFT
    angle = 2.0 * math.pi * phase.astype(F32) / NFFT
    weight = jnp.where(lag < WINDOW, taper, 0.0)[None, :]
    both = jnp.stack([weight * jnp.cos(angle), -weight * jnp.sin(angle)], axis=1)
    return both.astype(BF16).reshape(16, SAMPLES)


def lag_rows(offsets):
    tick = jnp.arange(SAMPLES, dtype=jnp.int32)
    lag = tick[None, :, None] - offsets.reshape(-1, 1, GROUP)
    return lag.reshape(-1, 1, SAMPLES * GROUP)


def spectra_kernel(steps_rows, place, table, lags, rows, cols, *refs):
    outs, weights, result = refs[:8], refs[8], refs[9]
    step = pl.program_id(0)
    zl = place[0]

    def stations(traces, group, width, store):
        lag = lags[pl.ds(step * (STEP // GROUP) + group, 1)].reshape(1, SAMPLES * GROUP)
        tick = lax.broadcasted_iota(jnp.int32, (SAMPLES, SAMPLES * GROUP), 0)
        onehot = jnp.where(tick == lag, 1.0, 0.0).astype(BF16)
        basis = jnp.dot(table[...], onehot, preferred_element_type=F32).astype(BF16)
        lane = lax.broadcasted_iota(jnp.int32, (16, SAMPLES * GROUP), 1) % GROUP
        for n in range(GROUP):
            mask = jnp.where(lane == n, 1.0, 0.0).astype(BF16)
            weights[pl.ds(n * 16, 16), :] = basis * mask
        block = traces[:, pl.ds(group * GROUP, GROUP), :]
        spectrum = jnp.dot(
            weights[...],
            block.reshape(SAMPLES * GROUP, width),
            preferred_element_type=F32,
        )
        for half in range(width // 128):
            result[half] = spectrum[:, half * 128:half * 128 + 128]
        for slot in range(8):
            for part in range(2):
                store(slot, part, pl.ds(slot * 2 + part, GROUP, 16))

    @pl.when(step < steps_rows)
    def _():
        for group in range(STEP // GROUP):
            first = step * STEP + group * GROUP

            def store(slot, part, picked):
                at = pl.multiple_of(part * 512 + first, GROUP)
                outs[slot][pl.ds(at, GROUP), :] = result[0, picked, :].astype(BF16)

            stations(rows, group, 128, store)

    @pl.when(step >= steps_rows)
    def _():
        for group in range(STEP // GROUP):
            first = (step - steps_rows) * STEP + group * GROUP

            def store(slot, part, picked):
                for half in range(2):
                    at = 1024 + (half ^ zl) * 512 + part * 256 + first
                    outs[slot][pl.ds(pl.multiple_of(at, GROUP), GROUP), :] = result[half, picked, :].astype(BF16)

            stations(cols, group, 256, store)


def spectra(place, table, lags, rows, cols):
    steps_rows, steps_cols = rows.shape[1] // STEP, cols.shape[1] // STEP
    whole = lambda *shape: pl.BlockSpec(shape, lambda s, _: (0,) * len(shape))
    return pl.pallas_call(
        functools.partial(spectra_kernel, steps_rows),
        grid_spec=pltpu.PrefetchScalarGridSpec(
            num_scalar_prefetch=1,
            grid=(steps_rows + steps_cols,),
            in_specs=[
                whole(16, SAMPLES),
                whole(*lags.shape),
                pl.BlockSpec((SAMPLES, STEP, 128), lambda s, _: (0, jnp.minimum(s, steps_rows - 1), 0)),
                pl.BlockSpec((SAMPLES, STEP, 256), lambda s, _: (0, jnp.maximum(s - steps_rows, 0), 0)),
            ],
            out_specs=[whole(2048, 128)] * 8,
            scratch_shapes=[
                pltpu.VMEM((256, SAMPLES * GROUP), BF16),
                pltpu.VMEM((2, 256, 128), F32),
            ],
        ),
        out_shape=[jax.ShapeDtypeStruct((2048, 128), BF16)] * 8,
        compiler_params=pltpu.CompilerParams(vmem_limit_bytes=48 << 20),
        cost_estimate=pl.CostEstimate(flops=4 << 30, bytes_accessed=20 << 20, transcendentals=0),
        name="spectra",
    )(place, table, lags, rows, cols)


def correlate_kernel(halves, swap, keep, has_start, place, *refs):
    count = 24
    pieces, refs = refs[:count], refs[count:]
    starts, refs = refs[: len(halves) * has_start], refs[len(halves) * has_start:]
    outs, refs = refs[: len(halves)], refs[len(halves):]
    a_all, b_all, sems = refs[:3]
    core = place[1]
    first = core == (1 if swap else 0)
    a_in = [pieces[0:4], pieces[4:8], pieces[8:12]]
    b_in = [pieces[12:16], pieces[16:20], pieces[20:24]]

    def copies(chunk, slot):
        got = []
        for n in range(4):
            got.append(pltpu.make_async_copy(a_in[chunk][n], a_all.at[place[2 + n], slot], sems.at[slot * 8 + n]))
            got.append(pltpu.make_async_copy(b_in[chunk][n], b_all.at[place[6 + n], slot], sems.at[slot * 8 + 4 + n]))
        return got

    for copy in copies(0, 0):
        copy.start()

    @pl.when(first)
    def _():
        for copy in copies(1, 1):
            copy.start()

    @pl.when(jnp.logical_not(first))
    def _():
        for copy in copies(2, 1):
            copy.start()

    for copy in copies(0, 0) + copies(1, 1):
        copy.wait()

    scale = 1.0 / K_AUX
    for at, half in enumerate(halves):
        out = outs[at]
        for part in range(2):

            def body(block, _):
                rows = pl.ds(pl.multiple_of(block * 256, 256), 256)
                total = starts[at][part, rows, :] if has_start else None
                for q in range(4):
                    left, right = [], []
                    for other in range(2):
                        for z in range(2):
                            for p in range(2):
                                left.append(a_all[q, z, other, p, rows, :])
                                b = b_all[q, half, other, z ^ half, p ^ part]
                                right.append(-b if part == 1 and p == 0 else b)
                    term = lax.dot_general(
                        jnp.concatenate(left, axis=1),
                        jnp.concatenate(right, axis=1),
                        (((1,), (1,)), ((), ())),
                        preferred_element_type=F32,
                    )
                    total = term if total is None else total + term
                if keep is None:
                    out[part, rows, :] = total
                elif keep:
                    out[0, part, rows, :] = total * scale
                else:
                    out[part, rows, :] = (total * scale).astype(BF16)
                return 0

            lax.fori_loop(0, 2, body, 0)


def correlate(place, a_chunks, b_chunks, halves, swap=False, keep=None, starts=()):
    pieces = [piece for chunk in a_chunks + b_chunks for piece in chunk]
    whole = lambda *shape: pl.BlockSpec(shape, lambda s, _: (0,) * len(shape))
    if keep is None:
        outs = [jax.ShapeDtypeStruct((2, 512, 256), F32)] * len(halves)
        out_specs = [whole(2, 512, 256)] * len(halves)
    elif keep:
        outs = [jax.ShapeDtypeStruct((2, 2, 512, 256), F32)]
        out_specs = [pl.BlockSpec((1, 2, 512, 256), lambda s, place: (place[0], 0, 0, 0))]
    else:
        outs = [jax.ShapeDtypeStruct((2, 512, 256), BF16)]
        out_specs = [whole(2, 512, 256)]
    return pl.pallas_call(
        functools.partial(correlate_kernel, halves, swap, keep, len(starts) > 0),
        grid_spec=pltpu.PrefetchScalarGridSpec(
            num_scalar_prefetch=1,
            grid=(1,),
            in_specs=[pl.BlockSpec(memory_space=pl.ANY)] * 24 + [whole(2, 512, 256)] * len(starts),
            out_specs=out_specs,
            scratch_shapes=[
                pltpu.VMEM((4, 2, 2, 2, 512, 128), BF16),
                pltpu.VMEM((4, 2, 2, 2, 2, 256, 128), BF16),
                pltpu.SemaphoreType.DMA((16,)),
            ],
        ),
        out_shape=outs,
        compiler_params=pltpu.CompilerParams(vmem_limit_bytes=48 << 20),
        cost_estimate=pl.CostEstimate(flops=(2 << 30) * len(halves), bytes_accessed=10 << 20, transcendentals=0),
        name="correlate",
    )(place, *pieces, *starts)


def finish_kernel(place, got, whole, out):
    del place, whole
    out[0] = got[...].astype(F32)


def finish(place, got, whole):
    return pl.pallas_call(
        finish_kernel,
        grid_spec=pltpu.PrefetchScalarGridSpec(
            num_scalar_prefetch=1,
            grid=(2,),
            in_specs=[
                pl.BlockSpec((1, 512, 256), lambda s, _: (s, 0, 0)),
                pl.BlockSpec(memory_space=pl.ANY),
            ],
            out_specs=pl.BlockSpec((1, 1, 512, 256), lambda s, place: (1 - place[0], s, 0, 0)),
        ),
        out_shape=jax.ShapeDtypeStruct((2, 2, 512, 256), F32),
        input_output_aliases={2: 0},
        name="finish",
    )(place, got, whole)


def local(traces_rows, traces_cols, offsets_rows, offsets_cols, bins):
    layer, x, col = (lax.axis_index(axis) for axis in AXES)
    y, zl, zh, core = col // 2, col % 2, layer // 2, layer % 2
    z = 2 * zh + zl
    one, three = 1 + 2 * core, 3 - 2 * core
    place = jnp.stack(
        [zl, core, y, y ^ one, y ^ three, y ^ 2, x, x ^ one, x ^ three, x ^ 2]
    ).astype(jnp.int32)

    dests = [
        (z, core), (z, 1 - core), (z ^ one, core), (z ^ three, 1 - core),
        (z ^ three, core), (z ^ one, 1 - core), (z ^ 2, core), (z ^ 2, 1 - core),
    ]
    order = jnp.stack([4 * (a // 2) + 2 * b + a % 2 for a, b in dests])
    picked = jnp.sum(jnp.where(order[:, None] == jnp.arange(8)[None, :], bins[None, :], 0), axis=1)
    lags = jnp.concatenate([lag_rows(offsets_rows), lag_rows(offsets_cols)], axis=0)
    own, *away = spectra(place, basis_table(picked), lags, traces_rows, traces_cols)

    got = [send(slab, pairs) for slab, pairs in zip(away, SLOTS)]
    pairs = [(own, got[0]), (got[1], got[2]), (got[3], got[4]), (got[5], got[6])]
    a_chunks, b_chunks = [], []
    for first, second in pairs:
        a = jnp.stack([first[:1024], second[:1024]]).reshape(2, 2, 512, 128)
        b = jnp.stack([first[1024:], second[1024:]]).reshape(2, 2, 2, 256, 128)
        for chunk, chunks, one_way, other_way in ((a, a_chunks, Y_A, Y_B), (b, b_chunks, X_A, X_B)):
            near_by, far_by = send(chunk, one_way), send(chunk, other_way)
            chunks.append((chunk, near_by, far_by, send(far_by, one_way)))

    pa, qa, ra, sa = a_chunks
    pb, qb, rb, sb = b_chunks
    keep0, send0 = correlate(place, [pa, qa, ra], [pb, qb, rb], (0, 1))
    (leaves,) = correlate(place, [sa, qa, ra], [sb, qb, rb], (1,), swap=True, keep=False, starts=(send0,))
    arrived = send(leaves, HALVES)
    (stays,) = correlate(place, [sa, qa, ra], [sb, qb, rb], (0,), swap=True, keep=True, starts=(keep0,))
    return finish(place, arrived, stays)


def solution(mesh):
    return jax.shard_map(
        local,
        mesh=mesh,
        in_specs=(
            P(None, "row", ("layer", "col")),
            P(None, "col", ("layer", "row")),
            P("row"),
            P("col"),
            P(),
        ),
        out_specs=P("layer", None, "row", "col"),
        check_vma=False,
    )
```

```python
import functools
import math

import jax
import jax.numpy as jnp
from jax import lax
from jax.experimental import pallas as pl
from jax.experimental.pallas import tpu as pltpu
from jax.sharding import PartitionSpec as P

NFFT = 1024
SAMPLES = 64
WINDOW = 48
K_AUX = 4096
AXES = ("layer", "row", "col")
GROUP = 16
STEP = 64
BF16 = jnp.bfloat16
F32 = jnp.float32


def permutation(dest):
    pairs = []
    for layer in range(4):
        for row in range(4):
            for col in range(8):
                z, core = 2 * (layer // 2) + col % 2, layer % 2
                x, y, z, core2 = dest(row, col // 2, z, core)
                to = ((z // 2) * 2 + core2) * 32 + x * 8 + y * 2 + z % 2
                pairs.append(((layer * 4 + row) * 8 + col, to))
    return pairs


def near(core):
    return 3 if core else 1


def far(core):
    return 1 if core else 3


Y_A = permutation(lambda x, y, z, c: (x, y ^ near(c), z, c))
Y_B = permutation(lambda x, y, z, c: (x, y ^ far(c), z, c))
X_A = permutation(lambda x, y, z, c: (x ^ near(c), y, z, c))
X_B = permutation(lambda x, y, z, c: (x ^ far(c), y, z, c))
SLOTS = [
    permutation(lambda x, y, z, c: (x, y, z, 1 - c)),
    permutation(lambda x, y, z, c: (x, y, z ^ near(c), c)),
    permutation(lambda x, y, z, c: (x, y, z ^ far(c), 1 - c)),
    permutation(lambda x, y, z, c: (x, y, z ^ far(c), c)),
    permutation(lambda x, y, z, c: (x, y, z ^ near(c), 1 - c)),
    permutation(lambda x, y, z, c: (x, y, z ^ 2, c)),
    permutation(lambda x, y, z, c: (x, y, z ^ 2, 1 - c)),
]
HALVES = permutation(lambda x, y, z, c: (x, y, z ^ 1, c))


LANES = (
    ("y1b", "y1f", "y2a"),
    ("y1a", "y2b", "y2f"),
    ("Bza", "Bzb", "Az2", "Bz2"),
    ("Bzbc", "Bzac", "Az2c", "Bz2c"),
    ("xPb", "xPf", "xQa", "xSb", "xSf"),
    ("xPa", "xQb", "xQf", "xSa"),
)
SLOT_NAMES = ("cc", "za", "zbc", "zb", "zac", "z2", "z2c")


def send(value, pairs):
    return lax.ppermute(value, AXES, pairs)


def after(value, *others):
    return lax.optimization_barrier((value,) + others)[0] if others else value


def basis_table(bins):
    lag = jnp.arange(SAMPLES, dtype=jnp.int32)
    taper = 0.5 - 0.5 * jnp.cos(2.0 * math.pi * (lag.astype(F32) + 0.5) / WINDOW)
    clipped = jnp.clip(lag, 0, WINDOW - 1)
    phase = bins[:, None] * clipped[None, :] % NFFT
    angle = 2.0 * math.pi * phase.astype(F32) / NFFT
    weight = jnp.where(lag < WINDOW, taper, 0.0)[None, :]
    both = jnp.stack([weight * jnp.cos(angle), -weight * jnp.sin(angle)], axis=1)
    return both.astype(BF16).reshape(16, SAMPLES)


def lag_rows(offsets):
    tick = jnp.arange(SAMPLES, dtype=jnp.int32)
    lag = tick[None, :, None] - offsets.reshape(-1, 1, GROUP)
    return lag.reshape(-1, 1, SAMPLES * GROUP)


def spectra_kernel(halves, place, table, lags, traces, *refs):
    outs, weights, result, masks = refs[:8], refs[8], refs[9], refs[10]
    step = pl.program_id(0)
    stations = lags.shape[0] * GROUP
    lanes = SAMPLES * GROUP

    @pl.when(step == 0)
    def _():
        lane = lax.broadcasted_iota(jnp.int32, (16, 128), 1) % GROUP
        for n in range(GROUP):
            masks[n] = jnp.where(lane == n, 1.0, 0.0).astype(BF16)

    def build(group):
        lag = lags[pl.ds(step * (STEP // GROUP) + group, 1)].reshape(1, lanes)
        tick = lax.broadcasted_iota(jnp.int32, (SAMPLES, lanes), 0)
        onehot = jnp.where(tick == lag, 1.0, 0.0).astype(BF16)
        basis = jnp.dot(table[...], onehot, preferred_element_type=F32).astype(BF16)
        for n in range(GROUP):
            mask = masks[n]
            for at in range(0, lanes, 128):
                weights[group, pl.ds(n * 16, 16), pl.ds(at, 128)] = basis[:, at:at + 128] * mask

    def multiply(group):
        block = traces[:, pl.ds(group * GROUP, GROUP), :].reshape(lanes, halves * 128)
        spectrum = jnp.dot(weights[group], block, preferred_element_type=F32)
        for half in range(halves):
            result[group, half] = spectrum[:, half * 128:half * 128 + 128]

    def store(group):
        first = step * STEP + group * GROUP
        for slot in range(8):
            for part in range(2):
                picked = pl.ds(slot * 2 + part, GROUP, 16)
                for half in range(halves):
                    base = (half ^ place[0]) * 2 * stations if halves == 2 else 0
                    at = pl.multiple_of(base + part * stations + first, GROUP)
                    outs[slot][pl.ds(at, GROUP), :] = result[group, half, picked, :].astype(BF16)

    groups = STEP // GROUP
    build(0)
    for group in range(groups):
        if group + 1 < groups:
            build(group + 1)
        multiply(group)
        if group:
            store(group - 1)
    store(groups - 1)


def spectra(place, table, lags, traces):
    stations, width = traces.shape[1:]
    rows = 2 * stations * (width // 128)
    whole = lambda *shape: pl.BlockSpec(shape, lambda s, _: (0,) * len(shape))
    return pl.pallas_call(
        functools.partial(spectra_kernel, width // 128),
        grid_spec=pltpu.PrefetchScalarGridSpec(
            num_scalar_prefetch=1,
            grid=(stations // STEP,),
            in_specs=[
                whole(16, SAMPLES),
                whole(*lags.shape),
                pl.BlockSpec((SAMPLES, STEP, width), lambda s, _: (0, s, 0)),
            ],
            out_specs=[whole(rows, 128)] * 8,
            scratch_shapes=[
                pltpu.VMEM((STEP // GROUP, 256, SAMPLES * GROUP), BF16),
                pltpu.VMEM((STEP // GROUP, width // 128, 256, 128), F32),
                pltpu.VMEM((GROUP, 16, 128), BF16),
            ],
        ),
        out_shape=[jax.ShapeDtypeStruct((rows, 128), BF16)] * 8,
        compiler_params=pltpu.CompilerParams(vmem_limit_bytes=48 << 20),
        cost_estimate=pl.CostEstimate(flops=8 << 30, bytes_accessed=10 << 20, transcendentals=0),
        name="spectra",
    )(place, table, lags, traces)


def correlate_kernel(pairs, picks, part_out, has_start, place, *refs):
    a_in, b_in, refs = refs[:4], refs[4:8], refs[8:]
    start, refs = (refs[0], refs[1:]) if has_start else (None, refs)
    out, a_all, b_all, total, a_sems, b_sems = refs
    core = place[1]
    entry = 0 if picks is None else 2 * jnp.where(core == 0, picks[0], picks[1])

    a_copies = [pltpu.make_async_copy(a_in[n], a_all.at[n], a_sems.at[n]) for n in range(4)]
    b_copies = [
        pltpu.make_async_copy(b_in[n].at[pl.ds(entry, 2)], b_all.at[place[6 + n]], b_sems.at[n])
        for n in range(4)
    ]
    for copy in b_copies + a_copies:
        copy.start()
    for copy in b_copies:
        copy.wait()

    scale = 1.0 / K_AUX
    for n in range(4):
        a_copies[n].wait()
        q = place[2 + n]
        for part in range(2):
            right = []
            for z, half in pairs:
                for other in range(2):
                    for p in range(2):
                        piece = b_all[q, other, half, p ^ part]
                        right.append(-piece if part == 1 and p == 0 else piece)
            right = jnp.concatenate(right, axis=1)
            for block in range(2):
                rows = pl.ds(block * 256, 256)
                left = [
                    a_all[n, 2 * z + other, p, rows, :]
                    for z, _ in pairs
                    for other in range(2)
                    for p in range(2)
                ]
                term = lax.dot_general(
                    jnp.concatenate(left, axis=1),
                    right,
                    (((1,), (1,)), ((), ())),
                    preferred_element_type=F32,
                )
                if n > 0:
                    term += total[part, rows, :]
                elif has_start:
                    term += start[part, rows, :]
                if n < 3:
                    total[part, rows, :] = term
                elif part_out == "sum":
                    out[part, rows, :] = term
                elif part_out == "send":
                    out[part, rows, :] = (term * scale).astype(BF16)
                else:
                    out[0, part, rows, :] = term * scale


def correlate(place, a_pieces, b_pieces, pairs, picks, part_out, start=None):
    whole = lambda *shape: pl.BlockSpec(shape, lambda s, _: (0,) * len(shape))
    out, out_spec = jax.ShapeDtypeStruct((2, 512, 256), F32), whole(2, 512, 256)
    if part_out == "send":
        out = jax.ShapeDtypeStruct((2, 512, 256), BF16)
    elif part_out == "keep":
        out = jax.ShapeDtypeStruct((2, 2, 512, 256), F32)
        out_spec = pl.BlockSpec((1, 2, 512, 256), lambda s, place: (place[0], 0, 0, 0))
    starts = [] if start is None else [start]
    return pl.pallas_call(
        functools.partial(correlate_kernel, pairs, picks, part_out, start is not None),
        grid_spec=pltpu.PrefetchScalarGridSpec(
            num_scalar_prefetch=1,
            grid=(1,),
            in_specs=[pl.BlockSpec(memory_space=pl.ANY)] * 8 + [whole(2, 512, 256)] * len(starts),
            out_specs=out_spec,
            scratch_shapes=[
                pltpu.VMEM((4, 4, 2, 512, 128), BF16),
                pltpu.VMEM((4, 2, 2, 2, 256, 128), BF16),
                pltpu.VMEM((2, 512, 256), F32),
                pltpu.SemaphoreType.DMA((4,)),
                pltpu.SemaphoreType.DMA((4,)),
            ],
        ),
        out_shape=out,
        compiler_params=pltpu.CompilerParams(vmem_limit_bytes=20 << 20),
        cost_estimate=pl.CostEstimate(
            flops=(32 if part_out == "send" else 2) << 30, bytes_accessed=6 << 20, transcendentals=0
        ),
        name="correlate",
    )(place, *a_pieces, *b_pieces, *starts)


KEEP = ((0, 0), (1, 1))
SEND = ((0, 1), (1, 0))


def finish_kernel(place, got, whole, out):
    del place, whole
    out[0] = got[...].astype(F32)


def finish(place, got, whole):
    return pl.pallas_call(
        finish_kernel,
        grid_spec=pltpu.PrefetchScalarGridSpec(
            num_scalar_prefetch=1,
            grid=(2,),
            in_specs=[
                pl.BlockSpec((1, 512, 256), lambda s, _: (s, 0, 0)),
                pl.BlockSpec(memory_space=pl.ANY),
            ],
            out_specs=pl.BlockSpec((1, 1, 512, 256), lambda s, place: (1 - place[0], s, 0, 0)),
        ),
        out_shape=jax.ShapeDtypeStruct((2, 2, 512, 256), F32),
        input_output_aliases={2: 0},
        name="finish",
    )(place, got, whole)


def local(traces_rows, traces_cols, offsets_rows, offsets_cols, bins):
    layer, x, col = (lax.axis_index(axis) for axis in AXES)
    y, zl, zh, core = col // 2, col % 2, layer // 2, layer % 2
    z = 2 * zh + zl
    one, three = 1 + 2 * core, 3 - 2 * core
    place = jnp.stack(
        [zl, core, y, y ^ one, y ^ three, y ^ 2, x, x ^ one, x ^ three, x ^ 2]
    ).astype(jnp.int32)

    dests = [
        (z, core), (z, 1 - core), (z ^ one, core), (z ^ three, 1 - core),
        (z ^ three, core), (z ^ one, 1 - core), (z ^ 2, core), (z ^ 2, 1 - core),
    ]
    order = jnp.stack([4 * (a // 2) + 2 * b + a % 2 for a, b in dests])
    picked = jnp.sum(jnp.where(order[:, None] == jnp.arange(8)[None, :], bins[None, :], 0), axis=1)
    table = basis_table(picked)
    a_own, *a_away = spectra(place, table, lag_rows(offsets_rows), traces_rows)
    b_own, *b_away = spectra(after(place, a_own), table, lag_rows(offsets_cols), traces_cols)

    slabs = {"A" + name: slab for name, slab in zip(SLOT_NAMES, a_away)}
    slabs.update({"B" + name: slab for name, slab in zip(SLOT_NAMES, b_away)})
    moves = {array + name: pairs for name, pairs in zip(SLOT_NAMES, SLOTS) for array in "AB"}
    moves.update(ya=Y_A, yb=Y_B, yf=Y_A, xa=X_A, xb=X_B, xf=X_A)
    before = {name: lane[n - 1] for lane in LANES for n, name in enumerate(lane) if n}
    got, chunks = {}, {}

    def build(name):
        axis, which = name
        array, own = ("A", a_own) if axis == "y" else ("B", b_own)
        slots = lambda *names: jnp.stack([arrival(array + n) for n in names])
        if axis == "y":
            q, r = slots("za", "zbc"), slots("zb", "zac")
            if which == "1":
                parts = [own[None], slots("cc"), jnp.where(core == 0, q, r)]
            else:
                parts = [slots("z2", "z2c"), jnp.where(core == 0, r, q)]
            return jnp.concatenate(parts).reshape(4, 2, 512, 128)
        if which == "P":
            parts = [own[None], slots("cc")]
        elif which == "Q":
            parts = [slots("za", "zbc", "zb", "zac")]
        else:
            parts = [slots("z2", "z2c")]
        return jnp.concatenate(parts).reshape(-1, 2, 2, 256, 128)

    def chunk(name):
        if name not in chunks:
            chunks[name] = build(name)
        return chunks[name]

    def arrival(name):
        if name not in got:
            if name in slabs:
                value, move = slabs[name], moves[name]
            else:
                which, way = name[:2], name[2]
                value = arrival(which + "b") if way == "f" else chunk(which)
                move = moves[name[0] + way]
            if name in before:
                value = after(value, arrival(before[name]))
            with jax.named_scope("send_" + name):
                got[name] = send(value, move)
        return got[name]

    pieces = {
        name: [chunk(name)] + [arrival(name + way) for way in "abf"] for name in ("y1", "y2", "xP", "xQ", "xS")
    }
    keep_early = correlate(place, pieces["y1"], pieces["xP"], KEEP, None, "sum")
    send_early = correlate(place, pieces["y1"], pieces["xQ"], SEND, (0, 1), "sum")
    leaves = correlate(place, pieces["y2"], pieces["xQ"], SEND, (1, 0), "send", send_early)
    arrived = send(leaves, HALVES)
    stays = correlate(after(place, leaves), pieces["y2"], pieces["xS"], KEEP, None, "keep", keep_early)
    return finish(place, arrived, stays)


def solution(mesh):
    return jax.shard_map(
        local,
        mesh=mesh,
        in_specs=(
            P(None, "row", ("layer", "col")),
            P(None, "col", ("layer", "row")),
            P("row"),
            P("col"),
            P(),
        ),
        out_specs=P("layer", None, "row", "col"),
        check_vma=False,
    )
```

```python
import functools
import math

import jax
import jax.numpy as jnp
from jax import lax
from jax.experimental import pallas as pl
from jax.experimental.pallas import tpu as pltpu
from jax.sharding import PartitionSpec as P

NFFT = 1024
SAMPLES = 64
WINDOW = 48
K_AUX = 4096
AXES = ("layer", "row", "col")
GROUP = 16
SUB = 8
STEP = 64
BF16 = jnp.bfloat16
F32 = jnp.float32


def permutation(dest):
    pairs = []
    for layer in range(4):
        for row in range(4):
            for col in range(8):
                z, core = 2 * (layer // 2) + col % 2, layer % 2
                x, y, z, core2 = dest(row, col // 2, z, core)
                to = ((z // 2) * 2 + core2) * 32 + x * 8 + y * 2 + z % 2
                pairs.append(((layer * 4 + row) * 8 + col, to))
    return pairs


def near(core):
    return 3 if core else 1


def far(core):
    return 1 if core else 3


Y_A = permutation(lambda x, y, z, c: (x, y ^ near(c), z, c))
Y_B = permutation(lambda x, y, z, c: (x, y ^ far(c), z, c))
X_A = permutation(lambda x, y, z, c: (x ^ near(c), y, z, c))
X_B = permutation(lambda x, y, z, c: (x ^ far(c), y, z, c))
SLOTS = [
    permutation(lambda x, y, z, c: (x, y, z, 1 - c)),
    permutation(lambda x, y, z, c: (x, y, z ^ near(c), c)),
    permutation(lambda x, y, z, c: (x, y, z ^ far(c), 1 - c)),
    permutation(lambda x, y, z, c: (x, y, z ^ far(c), c)),
    permutation(lambda x, y, z, c: (x, y, z ^ near(c), 1 - c)),
    permutation(lambda x, y, z, c: (x, y, z ^ 2, c)),
    permutation(lambda x, y, z, c: (x, y, z ^ 2, 1 - c)),
]
HALVES = permutation(lambda x, y, z, c: (x, y, z ^ 1, c))


LANES = (
    ("y1b", "y1f", "y2a"),
    ("y1a", "y2b", "y2f"),
    ("Bza", "Bzb", "Az2", "Bz2"),
    ("Bzbc", "Bzac", "Az2c", "Bz2c"),
    ("xPb", "xPf", "xQa", "xSb", "xSf"),
    ("xPa", "xQb", "xQf", "xSa"),
)
SLOT_NAMES = ("cc", "za", "zbc", "zb", "zac", "z2", "z2c")


def send(value, pairs):
    return lax.ppermute(value, AXES, pairs)


def after(value, *others):
    return lax.optimization_barrier((value,) + others)[0] if others else value


def basis_table(bins):
    lag = jnp.arange(SAMPLES, dtype=jnp.int32)
    taper = 0.5 - 0.5 * jnp.cos(2.0 * math.pi * (lag.astype(F32) + 0.5) / WINDOW)
    clipped = jnp.clip(lag, 0, WINDOW - 1)
    phase = bins[:, None] * clipped[None, :] % NFFT
    angle = 2.0 * math.pi * phase.astype(F32) / NFFT
    weight = jnp.where(lag < WINDOW, taper, 0.0)[None, :]
    both = jnp.stack([weight * jnp.cos(angle), -weight * jnp.sin(angle)], axis=1)
    return both.astype(BF16).reshape(16, SAMPLES)


def lag_rows(offsets):
    tick = jnp.arange(SAMPLES, dtype=jnp.int32)
    lag = tick[None, :, None] - offsets.reshape(-1, 1, SUB)
    return lag.reshape(-1, 1, SAMPLES * SUB)


def spectra_kernel(halves, place, table, lags, traces, *refs):
    outs, weights, result, masks = refs[:8], refs[8], refs[9], refs[10]
    step = pl.program_id(0)
    stations = lags.shape[0] * SUB
    lanes = SAMPLES * SUB

    @pl.when(step == 0)
    def _():
        lane = lax.broadcasted_iota(jnp.int32, (16, 128), 1) % SUB
        for n in range(SUB):
            masks[n] = jnp.where(lane == n, 1.0, 0.0).astype(BF16)

    def build(group):
        tick = lax.broadcasted_iota(jnp.int32, (SAMPLES, lanes), 0)
        for sub in range(GROUP // SUB):
            lag = lags[pl.ds(step * (STEP // SUB) + group * (GROUP // SUB) + sub, 1)].reshape(1, lanes)
            onehot = jnp.where(tick == lag, 1.0, 0.0).astype(BF16)
            basis = jnp.dot(table[...], onehot, preferred_element_type=F32).astype(BF16)
            for n in range(SUB):
                mask = masks[n]
                for at in range(0, lanes, 128):
                    weights[group, sub, pl.ds(n * 16, 16), pl.ds(at, 128)] = basis[:, at:at + 128] * mask

    def multiply(group):
        block = traces[:, pl.ds(group * GROUP, GROUP), :].astype(F32)
        for sub in range(GROUP // SUB):
            part = block[:, sub * SUB:(sub + 1) * SUB, :].reshape(lanes, halves * 128).astype(BF16)
            spectrum = jnp.dot(weights[group, sub], part, preferred_element_type=F32)
            for half in range(halves):
                result[group, half, pl.ds(sub * 128, 128), :] = spectrum[:, half * 128:half * 128 + 128]

    def store(group):
        first = step * STEP + group * GROUP
        for slot in range(8):
            for part in range(2):
                picked = pl.ds(slot * 2 + part, GROUP, 16)
                for half in range(halves):
                    base = (half ^ place[0]) * 2 * stations if halves == 2 else 0
                    at = pl.multiple_of(base + part * stations + first, GROUP)
                    outs[slot][pl.ds(at, GROUP), :] = result[group, half, picked, :].astype(BF16)

    groups = STEP // GROUP
    build(0)
    for group in range(groups):
        if group + 1 < groups:
            build(group + 1)
        multiply(group)
        if group:
            store(group - 1)
    store(groups - 1)


def spectra(place, table, lags, traces):
    stations, width = traces.shape[1:]
    rows = 2 * stations * (width // 128)
    whole = lambda *shape: pl.BlockSpec(shape, lambda s, _: (0,) * len(shape))
    return pl.pallas_call(
        functools.partial(spectra_kernel, width // 128),
        grid_spec=pltpu.PrefetchScalarGridSpec(
            num_scalar_prefetch=1,
            grid=(stations // STEP,),
            in_specs=[
                whole(16, SAMPLES),
                whole(*lags.shape),
                pl.BlockSpec((SAMPLES, STEP, width), lambda s, _: (0, s, 0)),
            ],
            out_specs=[whole(rows, 128)] * 8,
            scratch_shapes=[
                pltpu.VMEM((STEP // GROUP, GROUP // SUB, SUB * 16, SAMPLES * SUB), BF16),
                pltpu.VMEM((STEP // GROUP, width // 128, 256, 128), F32),
                pltpu.VMEM((SUB, 16, 128), BF16),
            ],
        ),
        out_shape=[jax.ShapeDtypeStruct((rows, 128), BF16)] * 8,
        compiler_params=pltpu.CompilerParams(vmem_limit_bytes=48 << 20),
        cost_estimate=pl.CostEstimate(flops=8 << 30, bytes_accessed=10 << 20, transcendentals=0),
        name="spectra",
    )(place, table, lags, traces)


def correlate_kernel(pairs, picks, part_out, has_start, place, *refs):
    a_in, b_in, refs = refs[:4], refs[4:8], refs[8:]
    start, refs = (refs[0], refs[1:]) if has_start else (None, refs)
    out, a_all, b_all, total, a_sems, b_sems = refs
    core = place[1]
    entry = 0 if picks is None else 2 * jnp.where(core == 0, picks[0], picks[1])

    a_copies = [pltpu.make_async_copy(a_in[n], a_all.at[n], a_sems.at[n]) for n in range(4)]
    b_copies = [
        pltpu.make_async_copy(b_in[n].at[pl.ds(entry, 2)], b_all.at[place[6 + n]], b_sems.at[n])
        for n in range(4)
    ]
    for copy in b_copies + a_copies:
        copy.start()
    for copy in b_copies:
        copy.wait()

    scale = 1.0 / K_AUX
    for n in range(4):
        a_copies[n].wait()
        q = place[2 + n]
        for part in range(2):
            right = []
            for z, half in pairs:
                for other in range(2):
                    for p in range(2):
                        piece = b_all[q, other, half, p ^ part]
                        right.append(-piece if part == 1 and p == 0 else piece)
            right = jnp.concatenate(right, axis=1)
            for block in range(2):
                rows = pl.ds(block * 256, 256)
                left = [
                    a_all[n, 2 * z + other, p, rows, :]
                    for z, _ in pairs
                    for other in range(2)
                    for p in range(2)
                ]
                term = lax.dot_general(
                    jnp.concatenate(left, axis=1),
                    right,
                    (((1,), (1,)), ((), ())),
                    preferred_element_type=F32,
                )
                if n > 0:
                    term += total[part, rows, :]
                elif has_start:
                    term += start[part, rows, :]
                if n < 3:
                    total[part, rows, :] = term
                elif part_out == "sum":
                    out[part, rows, :] = term
                elif part_out == "send":
                    out[part, rows, :] = (term * scale).astype(BF16)
                else:
                    out[0, part, rows, :] = term * scale


def correlate(place, a_pieces, b_pieces, pairs, picks, part_out, start=None):
    whole = lambda *shape: pl.BlockSpec(shape, lambda s, _: (0,) * len(shape))
    out, out_spec = jax.ShapeDtypeStruct((2, 512, 256), F32), whole(2, 512, 256)
    if part_out == "send":
        out = jax.ShapeDtypeStruct((2, 512, 256), BF16)
    elif part_out == "keep":
        out = jax.ShapeDtypeStruct((2, 2, 512, 256), F32)
        out_spec = pl.BlockSpec((1, 2, 512, 256), lambda s, place: (place[0], 0, 0, 0))
    starts = [] if start is None else [start]
    return pl.pallas_call(
        functools.partial(correlate_kernel, pairs, picks, part_out, start is not None),
        grid_spec=pltpu.PrefetchScalarGridSpec(
            num_scalar_prefetch=1,
            grid=(1,),
            in_specs=[pl.BlockSpec(memory_space=pl.ANY)] * 8 + [whole(2, 512, 256)] * len(starts),
            out_specs=out_spec,
            scratch_shapes=[
                pltpu.VMEM((4, 4, 2, 512, 128), BF16),
                pltpu.VMEM((4, 2, 2, 2, 256, 128), BF16),
                pltpu.VMEM((2, 512, 256), F32),
                pltpu.SemaphoreType.DMA((4,)),
                pltpu.SemaphoreType.DMA((4,)),
            ],
        ),
        out_shape=out,
        compiler_params=pltpu.CompilerParams(vmem_limit_bytes=20 << 20),
        cost_estimate=pl.CostEstimate(
            flops=(32 if part_out == "send" else 2) << 30, bytes_accessed=6 << 20, transcendentals=0
        ),
        name="correlate",
    )(place, *a_pieces, *b_pieces, *starts)


KEEP = ((0, 0), (1, 1))
SEND = ((0, 1), (1, 0))


def finish_kernel(got, whole, out, wide, sems):
    del whole
    slot = 1 - lax.axis_index("col") % 2
    copies = []
    for part in range(2):
        for half in range(2):
            rows = pl.ds(half * 256, 256)
            wide[part, rows, :] = got[part, rows, :].astype(F32)
            copies.append(
                pltpu.make_async_copy(
                    wide.at[part, rows], out.at[slot, part, rows], sems.at[2 * part + half]
                )
            )
            copies[-1].start()
    for copy in copies:
        copy.wait()


def finish(got, whole):
    return pl.pallas_call(
        finish_kernel,
        in_specs=[pl.BlockSpec(memory_space=pltpu.VMEM), pl.BlockSpec(memory_space=pl.ANY)],
        out_specs=pl.BlockSpec(memory_space=pl.ANY),
        scratch_shapes=[pltpu.VMEM((2, 512, 256), F32), pltpu.SemaphoreType.DMA((4,))],
        out_shape=jax.ShapeDtypeStruct((2, 2, 512, 256), F32),
        input_output_aliases={1: 0},
        name="finish",
    )(got, whole)


def local(traces_rows, traces_cols, offsets_rows, offsets_cols, bins):
    layer, x, col = (lax.axis_index(axis) for axis in AXES)
    y, zl, zh, core = col // 2, col % 2, layer // 2, layer % 2
    z = 2 * zh + zl
    one, three = 1 + 2 * core, 3 - 2 * core
    place = jnp.stack(
        [zl, core, y, y ^ one, y ^ three, y ^ 2, x, x ^ one, x ^ three, x ^ 2]
    ).astype(jnp.int32)

    dests = [
        (z, core), (z, 1 - core), (z ^ one, core), (z ^ three, 1 - core),
        (z ^ three, core), (z ^ one, 1 - core), (z ^ 2, core), (z ^ 2, 1 - core),
    ]
    order = jnp.stack([4 * (a // 2) + 2 * b + a % 2 for a, b in dests])
    picked = jnp.sum(jnp.where(order[:, None] == jnp.arange(8)[None, :], bins[None, :], 0), axis=1)
    table = basis_table(picked)
    a_own, *a_away = spectra(place, table, lag_rows(offsets_rows), traces_rows)
    b_own, *b_away = spectra(after(place, a_own), table, lag_rows(offsets_cols), traces_cols)

    slabs = {"A" + name: slab for name, slab in zip(SLOT_NAMES, a_away)}
    slabs.update({"B" + name: slab for name, slab in zip(SLOT_NAMES, b_away)})
    moves = {array + name: pairs for name, pairs in zip(SLOT_NAMES, SLOTS) for array in "AB"}
    moves.update(ya=Y_A, yb=Y_B, yf=Y_A, xa=X_A, xb=X_B, xf=X_A)
    before = {name: lane[n - 1] for lane in LANES for n, name in enumerate(lane) if n}
    got, chunks = {}, {}

    def build(name):
        axis, which = name
        array, own = ("A", a_own) if axis == "y" else ("B", b_own)
        slots = lambda *names: jnp.stack([arrival(array + n) for n in names])
        if axis == "y":
            q, r = slots("za", "zbc"), slots("zb", "zac")
            if which == "1":
                parts = [own[None], slots("cc"), jnp.where(core == 0, q, r)]
            else:
                parts = [slots("z2", "z2c"), jnp.where(core == 0, r, q)]
            return jnp.concatenate(parts).reshape(4, 2, 512, 128)
        if which == "P":
            parts = [own[None], slots("cc")]
        elif which == "Q":
            parts = [slots("za", "zbc", "zb", "zac")]
        else:
            parts = [slots("z2", "z2c")]
        return jnp.concatenate(parts).reshape(-1, 2, 2, 256, 128)

    def chunk(name):
        if name not in chunks:
            chunks[name] = build(name)
        return chunks[name]

    def arrival(name):
        if name not in got:
            if name in slabs:
                value, move = slabs[name], moves[name]
            else:
                which, way = name[:2], name[2]
                value = arrival(which + "b") if way == "f" else chunk(which)
                move = moves[name[0] + way]
            if name in before:
                value = after(value, arrival(before[name]))
            with jax.named_scope("send_" + name):
                got[name] = send(value, move)
        return got[name]

    pieces = {
        name: [chunk(name)] + [arrival(name + way) for way in "abf"] for name in ("y1", "y2", "xP", "xQ", "xS")
    }
    keep_early = correlate(place, pieces["y1"], pieces["xP"], KEEP, None, "sum")
    send_early = correlate(place, pieces["y1"], pieces["xQ"], SEND, (0, 1), "sum")
    leaves = correlate(place, pieces["y2"], pieces["xQ"], SEND, (1, 0), "send", send_early)
    arrived = send(leaves, HALVES)
    stays = correlate(after(place, leaves), pieces["y2"], pieces["xS"], KEEP, None, "keep", keep_early)
    return finish(arrived, stays)


def solution(mesh):
    return jax.shard_map(
        local,
        mesh=mesh,
        in_specs=(
            P(None, "row", ("layer", "col")),
            P(None, "col", ("layer", "row")),
            P("row"),
            P("col"),
            P(),
        ),
        out_specs=P("layer", None, "row", "col"),
        check_vma=False,
    )
```

```python
import functools
import math

import jax
import jax.numpy as jnp
from jax import lax
from jax.experimental import pallas as pl
from jax.experimental.pallas import tpu as pltpu
from jax.sharding import PartitionSpec as P

NFFT = 1024
SAMPLES = 64
WINDOW = 48
K_AUX = 4096
AXES = ("layer", "row", "col")
GROUP = 16
SUB = 8
STEP = 64
BF16 = jnp.bfloat16
F32 = jnp.float32


def permutation(dest):
    pairs = []
    for layer in range(4):
        for row in range(4):
            for col in range(8):
                z, core = 2 * (layer // 2) + col % 2, layer % 2
                x, y, z, core2 = dest(row, col // 2, z, core)
                to = ((z // 2) * 2 + core2) * 32 + x * 8 + y * 2 + z % 2
                pairs.append(((layer * 4 + row) * 8 + col, to))
    return pairs


def near(core):
    return 3 if core else 1


def far(core):
    return 1 if core else 3


Y_A = permutation(lambda x, y, z, c: (x, y ^ near(c), z, c))
Y_B = permutation(lambda x, y, z, c: (x, y ^ far(c), z, c))
X_A = permutation(lambda x, y, z, c: (x ^ near(c), y, z, c))
X_B = permutation(lambda x, y, z, c: (x ^ far(c), y, z, c))
SLOTS = [
    permutation(lambda x, y, z, c: (x, y, z, 1 - c)),
    permutation(lambda x, y, z, c: (x, y, z ^ near(c), c)),
    permutation(lambda x, y, z, c: (x, y, z ^ far(c), 1 - c)),
    permutation(lambda x, y, z, c: (x, y, z ^ far(c), c)),
    permutation(lambda x, y, z, c: (x, y, z ^ near(c), 1 - c)),
    permutation(lambda x, y, z, c: (x, y, z ^ 2, c)),
    permutation(lambda x, y, z, c: (x, y, z ^ 2, 1 - c)),
]
HALVES = permutation(lambda x, y, z, c: (x, y, z ^ 1, c))


LANES = (
    ("y1b", "y1f", "y2a"),
    ("y1a", "y2b", "y2f"),
    ("Bza", "Bzb", "Az2", "Bz2"),
    ("Bzbc", "Bzac", "Az2c", "Bz2c"),
    ("xPb", "xPf", "xQa", "xSb", "xSf"),
    ("xPa", "xQb", "xQf", "xSa"),
)
SLOT_NAMES = ("cc", "za", "zbc", "zb", "zac", "z2", "z2c")


def send(value, pairs):
    return lax.ppermute(value, AXES, pairs)


def after(value, *others):
    return lax.optimization_barrier((value,) + others)[0] if others else value


def basis_table(bins):
    lag = jnp.arange(SAMPLES, dtype=jnp.int32)
    taper = 0.5 - 0.5 * jnp.cos(2.0 * math.pi * (lag.astype(F32) + 0.5) / WINDOW)
    clipped = jnp.clip(lag, 0, WINDOW - 1)
    phase = bins[:, None] * clipped[None, :] % NFFT
    angle = 2.0 * math.pi * phase.astype(F32) / NFFT
    weight = jnp.where(lag < WINDOW, taper, 0.0)[None, :]
    both = jnp.stack([weight * jnp.cos(angle), -weight * jnp.sin(angle)], axis=1)
    return both.astype(BF16).reshape(16, SAMPLES)


def lag_rows(offsets):
    tick = jnp.arange(SAMPLES, dtype=jnp.int32)
    lag = tick[None, :, None] - offsets.reshape(-1, 1, SUB)
    return lag.reshape(-1, 1, SAMPLES * SUB)


def spectra_kernel(halves, place, table, lags, traces, *refs):
    outs, weights, result, masks = refs[:8], refs[8], refs[9], refs[10]
    step = pl.program_id(0)
    stations = lags.shape[0] * SUB
    lanes = SAMPLES * SUB

    @pl.when(step == 0)
    def _():
        lane = lax.broadcasted_iota(jnp.int32, (16, 128), 1) % SUB
        for n in range(SUB):
            masks[n] = jnp.where(lane == n, 1.0, 0.0).astype(BF16)

    def build(group):
        tick = lax.broadcasted_iota(jnp.int32, (SAMPLES, lanes), 0)
        for sub in range(GROUP // SUB):
            lag = lags[pl.ds(step * (STEP // SUB) + group * (GROUP // SUB) + sub, 1)].reshape(1, lanes)
            onehot = jnp.where(tick == lag, 1.0, 0.0).astype(BF16)
            basis = jnp.dot(table[...], onehot, preferred_element_type=F32).astype(BF16)
            for n in range(SUB):
                mask = masks[n]
                for at in range(0, lanes, 128):
                    weights[group, sub, pl.ds(n * 16, 16), pl.ds(at, 128)] = basis[:, at:at + 128] * mask

    def multiply(group):
        block = traces[:, pl.ds(group * GROUP, GROUP), :].astype(F32)
        for sub in range(GROUP // SUB):
            part = block[:, sub * SUB:(sub + 1) * SUB, :].reshape(lanes, halves * 128).astype(BF16)
            spectrum = jnp.dot(weights[group, sub], part, preferred_element_type=F32)
            for half in range(halves):
                result[group, half, pl.ds(sub * 128, 128), :] = spectrum[:, half * 128:half * 128 + 128]

    def store(group):
        first = step * STEP + group * GROUP
        for slot in range(8):
            for part in range(2):
                picked = pl.ds(slot * 2 + part, GROUP, 16)
                for half in range(halves):
                    base = (half ^ place[0]) * 2 * stations if halves == 2 else 0
                    at = pl.multiple_of(base + part * stations + first, GROUP)
                    outs[slot][pl.ds(at, GROUP), :] = result[group, half, picked, :].astype(BF16)

    groups = STEP // GROUP
    build(0)
    for group in range(groups):
        if group + 1 < groups:
            build(group + 1)
        multiply(group)
        if group:
            store(group - 1)
    store(groups - 1)


def spectra(place, table, lags, traces):
    stations, width = traces.shape[1:]
    rows = 2 * stations * (width // 128)
    whole = lambda *shape: pl.BlockSpec(shape, lambda s, _: (0,) * len(shape))
    return pl.pallas_call(
        functools.partial(spectra_kernel, width // 128),
        grid_spec=pltpu.PrefetchScalarGridSpec(
            num_scalar_prefetch=1,
            grid=(stations // STEP,),
            in_specs=[
                whole(16, SAMPLES),
                whole(*lags.shape),
                pl.BlockSpec((SAMPLES, STEP, width), lambda s, _: (0, s, 0)),
            ],
            out_specs=[whole(rows, 128)] * 8,
            scratch_shapes=[
                pltpu.VMEM((STEP // GROUP, GROUP // SUB, SUB * 16, SAMPLES * SUB), BF16),
                pltpu.VMEM((STEP // GROUP, width // 128, 256, 128), F32),
                pltpu.VMEM((SUB, 16, 128), BF16),
            ],
        ),
        out_shape=[jax.ShapeDtypeStruct((rows, 128), BF16)] * 8,
        compiler_params=pltpu.CompilerParams(vmem_limit_bytes=48 << 20),
        cost_estimate=pl.CostEstimate(flops=8 << 30, bytes_accessed=10 << 20, transcendentals=0),
        name="spectra",
    )(place, table, lags, traces)


def correlate_kernel(pairs, picks, parts, part_out, has_start, place, *refs):
    a_in, b_in, refs = refs[:4], refs[4:8], refs[8:]
    start, refs = (refs[0], refs[1:]) if has_start else (None, refs)
    out, a_all, b_all, total, a_sems, b_sems = refs
    core = place[1]
    entry = 0 if picks is None else 2 * jnp.where(core == 0, picks[0], picks[1])

    a_copies = [pltpu.make_async_copy(a_in[n], a_all.at[n], a_sems.at[n]) for n in range(4)]
    b_copies = [
        pltpu.make_async_copy(b_in[n].at[pl.ds(entry, 2)], b_all.at[place[6 + n]], b_sems.at[n])
        for n in range(4)
    ]
    for copy in b_copies + a_copies:
        copy.start()
    for copy in b_copies:
        copy.wait()

    scale = 1.0 / K_AUX
    for n in range(4):
        a_copies[n].wait()
        q = place[2 + n]
        for at, part in enumerate(parts):
            right = []
            for z, half in pairs:
                for other in range(2):
                    for p in range(2):
                        piece = b_all[q, other, half, p ^ part]
                        right.append(-piece if part == 1 and p == 0 else piece)
            right = jnp.concatenate(right, axis=1)
            for block in range(2):
                rows = pl.ds(block * 256, 256)
                left = [
                    a_all[n, 2 * z + other, p, rows, :]
                    for z, _ in pairs
                    for other in range(2)
                    for p in range(2)
                ]
                term = lax.dot_general(
                    jnp.concatenate(left, axis=1),
                    right,
                    (((1,), (1,)), ((), ())),
                    preferred_element_type=F32,
                )
                if n > 0:
                    term += total[at, rows, :]
                elif has_start:
                    term += start[at, rows, :]
                if n < 3:
                    total[at, rows, :] = term
                elif part_out == "sum":
                    out[at, rows, :] = term
                elif part_out == "send":
                    out[at, rows, :] = (term * scale).astype(BF16)
                else:
                    out[0, at, rows, :] = term * scale


def correlate(place, a_pieces, b_pieces, pairs, picks, part_out, start=None, parts=(0, 1)):
    whole = lambda *shape: pl.BlockSpec(shape, lambda s, _: (0,) * len(shape))
    out, out_spec = jax.ShapeDtypeStruct((2, 512, 256), F32), whole(2, 512, 256)
    if part_out == "send":
        out, out_spec = jax.ShapeDtypeStruct((len(parts), 512, 256), BF16), whole(len(parts), 512, 256)
    elif part_out == "keep":
        out = jax.ShapeDtypeStruct((2, 2, 512, 256), F32)
        out_spec = pl.BlockSpec((1, 2, 512, 256), lambda s, place: (place[0], 0, 0, 0))
    starts = [] if start is None else [start]
    return pl.pallas_call(
        functools.partial(correlate_kernel, pairs, picks, parts, part_out, start is not None),
        grid_spec=pltpu.PrefetchScalarGridSpec(
            num_scalar_prefetch=1,
            grid=(1,),
            in_specs=[pl.BlockSpec(memory_space=pl.ANY)] * 8
            + [pl.BlockSpec((len(parts), 512, 256), lambda s, _: (parts[0] // len(parts), 0, 0))] * len(starts),
            out_specs=out_spec,
            scratch_shapes=[
                pltpu.VMEM((4, 4, 2, 512, 128), BF16),
                pltpu.VMEM((4, 2, 2, 2, 256, 128), BF16),
                pltpu.VMEM((2, 512, 256), F32),
                pltpu.SemaphoreType.DMA((4,)),
                pltpu.SemaphoreType.DMA((4,)),
            ],
        ),
        out_shape=out,
        compiler_params=pltpu.CompilerParams(vmem_limit_bytes=20 << 20),
        cost_estimate=pl.CostEstimate(
            flops=(32 if part_out == "send" else 2) << 30, bytes_accessed=6 << 20, transcendentals=0
        ),
        name="correlate",
    )(place, *a_pieces, *b_pieces, *starts)


KEEP = ((0, 0), (1, 1))
SEND = ((0, 1), (1, 0))


def finish_kernel(to, got, whole, out, narrow, wide, in_sems, out_sems):
    del whole
    slot = 1 - lax.axis_index("col") % 2
    blocks = [(part, pl.ds(half * 256, 256)) for part in range(got.shape[0]) for half in range(2)]
    ins = [
        pltpu.make_async_copy(got.at[part, rows], narrow.at[part, rows], in_sems.at[n])
        for n, (part, rows) in enumerate(blocks)
    ]
    outs = [
        pltpu.make_async_copy(wide.at[part, rows], out.at[slot, to + part, rows], out_sems.at[n])
        for n, (part, rows) in enumerate(blocks)
    ]
    for copy in ins:
        copy.start()
    for n, (part, rows) in enumerate(blocks):
        ins[n].wait()
        wide[part, rows, :] = narrow[part, rows, :].astype(F32)
        outs[n].start()
    for copy in outs:
        copy.wait()


def finish(got, whole, part):
    return pl.pallas_call(
        functools.partial(finish_kernel, part),
        in_specs=[pl.BlockSpec(memory_space=pl.ANY)] * 2,
        out_specs=pl.BlockSpec(memory_space=pl.ANY),
        scratch_shapes=[
            pltpu.VMEM(got.shape, BF16),
            pltpu.VMEM(got.shape, F32),
            pltpu.SemaphoreType.DMA((2,)),
            pltpu.SemaphoreType.DMA((2,)),
        ],
        out_shape=jax.ShapeDtypeStruct((2, 2, 512, 256), F32),
        input_output_aliases={1: 0},
        compiler_params=pltpu.CompilerParams(vmem_limit_bytes=8 << 20),
        name="finish",
    )(got, whole)


def local(traces_rows, traces_cols, offsets_rows, offsets_cols, bins):
    layer, x, col = (lax.axis_index(axis) for axis in AXES)
    y, zl, zh, core = col // 2, col % 2, layer // 2, layer % 2
    z = 2 * zh + zl
    one, three = 1 + 2 * core, 3 - 2 * core
    place = jnp.stack(
        [zl, core, y, y ^ one, y ^ three, y ^ 2, x, x ^ one, x ^ three, x ^ 2]
    ).astype(jnp.int32)

    dests = [
        (z, core), (z, 1 - core), (z ^ one, core), (z ^ three, 1 - core),
        (z ^ three, core), (z ^ one, 1 - core), (z ^ 2, core), (z ^ 2, 1 - core),
    ]
    order = jnp.stack([4 * (a // 2) + 2 * b + a % 2 for a, b in dests])
    picked = jnp.sum(jnp.where(order[:, None] == jnp.arange(8)[None, :], bins[None, :], 0), axis=1)
    table = basis_table(picked)
    a_own, *a_away = spectra(place, table, lag_rows(offsets_rows), traces_rows)
    b_own, *b_away = spectra(after(place, a_own), table, lag_rows(offsets_cols), traces_cols)

    slabs = {"A" + name: slab for name, slab in zip(SLOT_NAMES, a_away)}
    slabs.update({"B" + name: slab for name, slab in zip(SLOT_NAMES, b_away)})
    moves = {array + name: pairs for name, pairs in zip(SLOT_NAMES, SLOTS) for array in "AB"}
    moves.update(ya=Y_A, yb=Y_B, yf=Y_A, xa=X_A, xb=X_B, xf=X_A)
    before = {name: lane[n - 1] for lane in LANES for n, name in enumerate(lane) if n}
    got, chunks = {}, {}

    def build(name):
        axis, which = name
        array, own = ("A", a_own) if axis == "y" else ("B", b_own)
        slots = lambda *names: jnp.stack([arrival(array + n) for n in names])
        if axis == "y":
            q, r = slots("za", "zbc"), slots("zb", "zac")
            if which == "1":
                parts = [own[None], slots("cc"), jnp.where(core == 0, q, r)]
            else:
                parts = [slots("z2", "z2c"), jnp.where(core == 0, r, q)]
            return jnp.concatenate(parts).reshape(4, 2, 512, 128)
        if which == "P":
            parts = [own[None], slots("cc")]
        elif which == "Q":
            parts = [slots("za", "zbc", "zb", "zac")]
        else:
            parts = [slots("z2", "z2c")]
        return jnp.concatenate(parts).reshape(-1, 2, 2, 256, 128)

    def chunk(name):
        if name not in chunks:
            chunks[name] = build(name)
        return chunks[name]

    def arrival(name):
        if name not in got:
            if name in slabs:
                value, move = slabs[name], moves[name]
            else:
                which, way = name[:2], name[2]
                value = arrival(which + "b") if way == "f" else chunk(which)
                move = moves[name[0] + way]
            if name in before:
                value = after(value, arrival(before[name]))
            with jax.named_scope("send_" + name):
                got[name] = send(value, move)
        return got[name]

    pieces = {
        name: [chunk(name)] + [arrival(name + way) for way in "abf"] for name in ("y1", "y2", "xP", "xQ", "xS")
    }
    keep_early = correlate(place, pieces["y1"], pieces["xP"], KEEP, None, "sum")
    send_early = correlate(place, pieces["y1"], pieces["xQ"], SEND, (0, 1), "sum")
    arrived, wait = [], (keep_early,)
    for part in range(2):
        leaves = correlate(
            after(place, *wait), pieces["y2"], pieces["xQ"], SEND, (1, 0), "send", send_early, (part,)
        )
        arrived.append(send(leaves, HALVES))
        wait = (leaves,)
    stays = correlate(after(place, leaves), pieces["y2"], pieces["xS"], KEEP, None, "keep", keep_early)
    for part, half in enumerate(arrived):
        stays = finish(half, stays, part)
    return stays


def solution(mesh):
    return jax.shard_map(
        local,
        mesh=mesh,
        in_specs=(
            P(None, "row", ("layer", "col")),
            P(None, "col", ("layer", "row")),
            P("row"),
            P("col"),
            P(),
        ),
        out_specs=P("layer", None, "row", "col"),
        check_vma=False,
    )
```

```python
import functools
import math

import jax
import jax.numpy as jnp
from jax import lax
from jax.experimental import pallas as pl
from jax.experimental.pallas import tpu as pltpu
from jax.sharding import PartitionSpec as P

NFFT = 1024
SAMPLES = 64
WINDOW = 48
K_AUX = 4096
AXES = ("layer", "row", "col")
GROUP = 16
SUB = 8
STEP = 128
BF16 = jnp.bfloat16
F32 = jnp.float32


def permutation(dest):
    pairs = []
    for layer in range(4):
        for row in range(4):
            for col in range(8):
                z, core = 2 * (layer // 2) + col % 2, layer % 2
                x, y, z, core2 = dest(row, col // 2, z, core)
                to = ((z // 2) * 2 + core2) * 32 + x * 8 + y * 2 + z % 2
                pairs.append(((layer * 4 + row) * 8 + col, to))
    return pairs


def near(core):
    return 3 if core else 1


def far(core):
    return 1 if core else 3


Y_A = permutation(lambda x, y, z, c: (x, y ^ near(c), z, c))
Y_B = permutation(lambda x, y, z, c: (x, y ^ far(c), z, c))
X_A = permutation(lambda x, y, z, c: (x ^ near(c), y, z, c))
X_B = permutation(lambda x, y, z, c: (x ^ far(c), y, z, c))
SLOTS = [
    permutation(lambda x, y, z, c: (x, y, z, 1 - c)),
    permutation(lambda x, y, z, c: (x, y, z ^ near(c), c)),
    permutation(lambda x, y, z, c: (x, y, z ^ far(c), 1 - c)),
    permutation(lambda x, y, z, c: (x, y, z ^ far(c), c)),
    permutation(lambda x, y, z, c: (x, y, z ^ near(c), 1 - c)),
    permutation(lambda x, y, z, c: (x, y, z ^ 2, c)),
    permutation(lambda x, y, z, c: (x, y, z ^ 2, 1 - c)),
]
HALVES = permutation(lambda x, y, z, c: (x, y, z ^ 1, c))


LANES = (
    ("y1b", "y1f", "y2a"),
    ("y1a", "y2b", "y2f"),
    ("Bza", "Bzb", "Az2", "Bz2"),
    ("Bzbc", "Bzac", "Az2c", "Bz2c"),
    ("xPb", "xPf", "xQa", "xSb", "xSf"),
    ("xPa", "xQb", "xQf", "xSa"),
)
SLOT_NAMES = ("cc", "za", "zbc", "zb", "zac", "z2", "z2c")


def send(value, pairs):
    return lax.ppermute(value, AXES, pairs)


def after(value, *others):
    return lax.optimization_barrier((value,) + others)[0] if others else value


def basis_table(bins):
    lag = jnp.arange(SAMPLES, dtype=jnp.int32)
    taper = 0.5 - 0.5 * jnp.cos(2.0 * math.pi * (lag.astype(F32) + 0.5) / WINDOW)
    clipped = jnp.clip(lag, 0, WINDOW - 1)
    phase = bins[:, None] * clipped[None, :] % NFFT
    angle = 2.0 * math.pi * phase.astype(F32) / NFFT
    weight = jnp.where(lag < WINDOW, taper, 0.0)[None, :]
    both = jnp.stack([weight * jnp.cos(angle), -weight * jnp.sin(angle)], axis=1)
    return both.astype(BF16).reshape(16, SAMPLES)


def lag_rows(offsets):
    tick = jnp.arange(SAMPLES, dtype=jnp.int32)
    lag = tick[None, :, None] - offsets.reshape(-1, 1, SUB)
    return lag.reshape(-1, 1, SAMPLES * SUB)


def spectra_kernel(halves, place, table, lags, traces, *refs):
    outs, weights, result, masks = refs[:8], refs[8], refs[9], refs[10]
    step = pl.program_id(0)
    stations = lags.shape[0] * SUB
    lanes = SAMPLES * SUB

    @pl.when(step == 0)
    def _():
        lane = lax.broadcasted_iota(jnp.int32, (16, 128), 1) % SUB
        for n in range(SUB):
            masks[n] = jnp.where(lane == n, 1.0, 0.0).astype(BF16)

    def build(group):
        tick = lax.broadcasted_iota(jnp.int32, (SAMPLES, lanes), 0)
        for sub in range(GROUP // SUB):
            lag = lags[pl.ds(step * (STEP // SUB) + group * (GROUP // SUB) + sub, 1)].reshape(1, lanes)
            onehot = jnp.where(tick == lag, 1.0, 0.0).astype(BF16)
            basis = jnp.dot(table[...], onehot, preferred_element_type=F32).astype(BF16)
            for n in range(SUB):
                mask = masks[n]
                for at in range(0, lanes, 128):
                    weights[group, sub, pl.ds(n * 16, 16), pl.ds(at, 128)] = basis[:, at:at + 128] * mask

    def multiply(group):
        block = traces[:, pl.ds(group * GROUP, GROUP), :].astype(F32)
        for sub in range(GROUP // SUB):
            part = block[:, sub * SUB:(sub + 1) * SUB, :].reshape(lanes, halves * 128).astype(BF16)
            spectrum = jnp.dot(weights[group, sub], part, preferred_element_type=F32)
            for half in range(halves):
                result[group, half, pl.ds(sub * 128, 128), :] = spectrum[:, half * 128:half * 128 + 128]

    def store(group):
        first = step * STEP + group * GROUP
        for slot in range(8):
            for part in range(2):
                picked = pl.ds(slot * 2 + part, GROUP, 16)
                for half in range(halves):
                    base = (half ^ place[0]) * 2 * stations if halves == 2 else 0
                    at = pl.multiple_of(base + part * stations + first, GROUP)
                    outs[slot][pl.ds(at, GROUP), :] = result[group, half, picked, :].astype(BF16)

    groups = STEP // GROUP
    build(0)
    for group in range(groups):
        if group + 1 < groups:
            build(group + 1)
        multiply(group)
        if group:
            store(group - 1)
    store(groups - 1)


def spectra(place, table, lags, traces):
    stations, width = traces.shape[1:]
    rows = 2 * stations * (width // 128)
    whole = lambda *shape: pl.BlockSpec(shape, lambda s, _: (0,) * len(shape))
    return pl.pallas_call(
        functools.partial(spectra_kernel, width // 128),
        grid_spec=pltpu.PrefetchScalarGridSpec(
            num_scalar_prefetch=1,
            grid=(stations // STEP,),
            in_specs=[
                whole(16, SAMPLES),
                whole(*lags.shape),
                pl.BlockSpec((SAMPLES, STEP, width), lambda s, _: (0, s, 0)),
            ],
            out_specs=[whole(rows, 128)] * 8,
            scratch_shapes=[
                pltpu.VMEM((STEP // GROUP, GROUP // SUB, SUB * 16, SAMPLES * SUB), BF16),
                pltpu.VMEM((STEP // GROUP, width // 128, 256, 128), F32),
                pltpu.VMEM((SUB, 16, 128), BF16),
            ],
        ),
        out_shape=[jax.ShapeDtypeStruct((rows, 128), BF16)] * 8,
        compiler_params=pltpu.CompilerParams(vmem_limit_bytes=48 << 20),
        cost_estimate=pl.CostEstimate(flops=8 << 30, bytes_accessed=10 << 20, transcendentals=0),
        name="spectra",
    )(place, table, lags, traces)


def correlate_kernel(pairs, picks, parts, part_out, has_start, place, *refs):
    a_in, b_in, refs = refs[:4], refs[4:8], refs[8:]
    start, refs = (refs[0], refs[1:]) if has_start else (None, refs)
    out, a_all, b_all, total, a_sems, b_sems = refs
    core = place[1]
    entry = 0 if picks is None else 2 * jnp.where(core == 0, picks[0], picks[1])

    a_copies = [pltpu.make_async_copy(a_in[n], a_all.at[n], a_sems.at[n]) for n in range(4)]
    b_copies = [
        pltpu.make_async_copy(b_in[n].at[pl.ds(entry, 2)], b_all.at[place[6 + n]], b_sems.at[n])
        for n in range(4)
    ]
    for copy in b_copies + a_copies:
        copy.start()
    for copy in b_copies:
        copy.wait()

    scale = 1.0 / K_AUX
    for n in range(4):
        a_copies[n].wait()
        q = place[2 + n]
        for at, part in enumerate(parts):
            right = []
            for z, half in pairs:
                for other in range(2):
                    for p in range(2):
                        piece = b_all[q, other, half, p ^ part]
                        right.append(-piece if part == 1 and p == 0 else piece)
            right = jnp.concatenate(right, axis=1)
            for block in range(2):
                rows = pl.ds(block * 256, 256)
                left = [
                    a_all[n, 2 * z + other, p, rows, :]
                    for z, _ in pairs
                    for other in range(2)
                    for p in range(2)
                ]
                term = lax.dot_general(
                    jnp.concatenate(left, axis=1),
                    right,
                    (((1,), (1,)), ((), ())),
                    preferred_element_type=F32,
                )
                if n > 0:
                    term += total[at, rows, :]
                elif has_start:
                    term += start[at, rows, :]
                if n < 3:
                    total[at, rows, :] = term
                elif part_out == "sum":
                    out[at, rows, :] = term
                elif part_out == "send":
                    out[at, rows, :] = (term * scale).astype(BF16)
                else:
                    out[0, at, rows, :] = term * scale


def correlate(place, a_pieces, b_pieces, pairs, picks, part_out, start=None, parts=(0, 1)):
    whole = lambda *shape: pl.BlockSpec(shape, lambda s, _: (0,) * len(shape))
    out, out_spec = jax.ShapeDtypeStruct((2, 512, 256), F32), whole(2, 512, 256)
    if part_out == "send":
        out, out_spec = jax.ShapeDtypeStruct((len(parts), 512, 256), BF16), whole(len(parts), 512, 256)
    elif part_out == "keep":
        out = jax.ShapeDtypeStruct((2, 2, 512, 256), F32)
        out_spec = pl.BlockSpec((1, 2, 512, 256), lambda s, place: (place[0], 0, 0, 0))
    starts = [] if start is None else [start]
    return pl.pallas_call(
        functools.partial(correlate_kernel, pairs, picks, parts, part_out, start is not None),
        grid_spec=pltpu.PrefetchScalarGridSpec(
            num_scalar_prefetch=1,
            grid=(1,),
            in_specs=[pl.BlockSpec(memory_space=pl.ANY)] * 8
            + [pl.BlockSpec((len(parts), 512, 256), lambda s, _: (parts[0] // len(parts), 0, 0))] * len(starts),
            out_specs=out_spec,
            scratch_shapes=[
                pltpu.VMEM((4, 4, 2, 512, 128), BF16),
                pltpu.VMEM((4, 2, 2, 2, 256, 128), BF16),
                pltpu.VMEM((2, 512, 256), F32),
                pltpu.SemaphoreType.DMA((4,)),
                pltpu.SemaphoreType.DMA((4,)),
            ],
        ),
        out_shape=out,
        compiler_params=pltpu.CompilerParams(vmem_limit_bytes=20 << 20),
        cost_estimate=pl.CostEstimate(
            flops=(32 if part_out == "send" else 2) << 30, bytes_accessed=6 << 20, transcendentals=0
        ),
        name="correlate",
    )(place, *a_pieces, *b_pieces, *starts)


KEEP = ((0, 0), (1, 1))
SEND = ((0, 1), (1, 0))


def finish_kernel(to, got, whole, out, narrow, wide, in_sems, out_sems):
    del whole
    slot = 1 - lax.axis_index("col") % 2
    blocks = [(part, pl.ds(half * 256, 256)) for part in range(got.shape[0]) for half in range(2)]
    ins = [
        pltpu.make_async_copy(got.at[part, rows], narrow.at[part, rows], in_sems.at[n])
        for n, (part, rows) in enumerate(blocks)
    ]
    outs = [
        pltpu.make_async_copy(wide.at[part, rows], out.at[slot, to + part, rows], out_sems.at[n])
        for n, (part, rows) in enumerate(blocks)
    ]
    for copy in ins:
        copy.start()
    for n, (part, rows) in enumerate(blocks):
        ins[n].wait()
        wide[part, rows, :] = narrow[part, rows, :].astype(F32)
        outs[n].start()
    for copy in outs:
        copy.wait()


def finish(got, whole, part):
    return pl.pallas_call(
        functools.partial(finish_kernel, part),
        in_specs=[pl.BlockSpec(memory_space=pl.ANY)] * 2,
        out_specs=pl.BlockSpec(memory_space=pl.ANY),
        scratch_shapes=[
            pltpu.VMEM(got.shape, BF16),
            pltpu.VMEM(got.shape, F32),
            pltpu.SemaphoreType.DMA((2,)),
            pltpu.SemaphoreType.DMA((2,)),
        ],
        out_shape=jax.ShapeDtypeStruct((2, 2, 512, 256), F32),
        input_output_aliases={1: 0},
        compiler_params=pltpu.CompilerParams(vmem_limit_bytes=8 << 20),
        name="finish",
    )(got, whole)


def local(traces_rows, traces_cols, offsets_rows, offsets_cols, bins):
    layer, x, col = (lax.axis_index(axis) for axis in AXES)
    y, zl, zh, core = col // 2, col % 2, layer // 2, layer % 2
    z = 2 * zh + zl
    one, three = 1 + 2 * core, 3 - 2 * core
    place = jnp.stack(
        [zl, core, y, y ^ one, y ^ three, y ^ 2, x, x ^ one, x ^ three, x ^ 2]
    ).astype(jnp.int32)

    dests = [
        (z, core), (z, 1 - core), (z ^ one, core), (z ^ three, 1 - core),
        (z ^ three, core), (z ^ one, 1 - core), (z ^ 2, core), (z ^ 2, 1 - core),
    ]
    order = jnp.stack([4 * (a // 2) + 2 * b + a % 2 for a, b in dests])
    picked = jnp.sum(jnp.where(order[:, None] == jnp.arange(8)[None, :], bins[None, :], 0), axis=1)
    table = basis_table(picked)
    a_own, *a_away = spectra(place, table, lag_rows(offsets_rows), traces_rows)
    b_own, *b_away = spectra(after(place, a_own), table, lag_rows(offsets_cols), traces_cols)

    slabs = {"A" + name: slab for name, slab in zip(SLOT_NAMES, a_away)}
    slabs.update({"B" + name: slab for name, slab in zip(SLOT_NAMES, b_away)})
    moves = {array + name: pairs for name, pairs in zip(SLOT_NAMES, SLOTS) for array in "AB"}
    moves.update(ya=Y_A, yb=Y_B, yf=Y_A, xa=X_A, xb=X_B, xf=X_A)
    before = {name: lane[n - 1] for lane in LANES for n, name in enumerate(lane) if n}
    got, chunks = {}, {}

    def build(name):
        axis, which = name
        array, own = ("A", a_own) if axis == "y" else ("B", b_own)
        slots = lambda *names: jnp.stack([arrival(array + n) for n in names])
        if axis == "y":
            q, r = slots("za", "zbc"), slots("zb", "zac")
            if which == "1":
                parts = [own[None], slots("cc"), jnp.where(core == 0, q, r)]
            else:
                parts = [slots("z2", "z2c"), jnp.where(core == 0, r, q)]
            return jnp.concatenate(parts).reshape(4, 2, 512, 128)
        if which == "P":
            parts = [own[None], slots("cc")]
        elif which == "Q":
            parts = [slots("za", "zbc", "zb", "zac")]
        else:
            parts = [slots("z2", "z2c")]
        return jnp.concatenate(parts).reshape(-1, 2, 2, 256, 128)

    def chunk(name):
        if name not in chunks:
            chunks[name] = build(name)
        return chunks[name]

    def arrival(name):
        if name not in got:
            if name in slabs:
                value, move = slabs[name], moves[name]
            else:
                which, way = name[:2], name[2]
                value = arrival(which + "b") if way == "f" else chunk(which)
                move = moves[name[0] + way]
            if name in before:
                value = after(value, arrival(before[name]))
            with jax.named_scope("send_" + name):
                got[name] = send(value, move)
        return got[name]

    pieces = {
        name: [chunk(name)] + [arrival(name + way) for way in "abf"] for name in ("y1", "y2", "xP", "xQ", "xS")
    }
    keep_early = correlate(place, pieces["y1"], pieces["xP"], KEEP, None, "sum")
    send_early = correlate(place, pieces["y1"], pieces["xQ"], SEND, (0, 1), "sum")
    arrived, wait = [], (keep_early,)
    for part in range(2):
        leaves = correlate(
            after(place, *wait), pieces["y2"], pieces["xQ"], SEND, (1, 0), "send", send_early, (part,)
        )
        arrived.append(send(leaves, HALVES))
        wait = (leaves,)
    stays = correlate(after(place, leaves), pieces["y2"], pieces["xS"], KEEP, None, "keep", keep_early)
    for part, half in enumerate(arrived):
        stays = finish(half, stays, part)
    return stays


def solution(mesh):
    return jax.shard_map(
        local,
        mesh=mesh,
        in_specs=(
            P(None, "row", ("layer", "col")),
            P(None, "col", ("layer", "row")),
            P("row"),
            P("col"),
            P(),
        ),
        out_specs=P("layer", None, "row", "col"),
        check_vma=False,
    )
```

```python
import functools
import math

import jax
import jax.numpy as jnp
from jax import lax
from jax.experimental import pallas as pl
from jax.experimental.pallas import tpu as pltpu
from jax.sharding import PartitionSpec as P

NFFT = 1024
SAMPLES = 64
WINDOW = 48
K_AUX = 4096
AXES = ("layer", "row", "col")
GROUP = 16
SUB = 8
STEP = 128
BF16 = jnp.bfloat16
F32 = jnp.float32


def permutation(dest):
    pairs = []
    for layer in range(4):
        for row in range(4):
            for col in range(8):
                z, core = 2 * (layer // 2) + col % 2, layer % 2
                x, y, z, core2 = dest(row, col // 2, z, core)
                to = ((z // 2) * 2 + core2) * 32 + x * 8 + y * 2 + z % 2
                pairs.append(((layer * 4 + row) * 8 + col, to))
    return pairs


def near(core):
    return 3 if core else 1


def far(core):
    return 1 if core else 3


Y_A = permutation(lambda x, y, z, c: (x, y ^ near(c), z, c))
Y_B = permutation(lambda x, y, z, c: (x, y ^ far(c), z, c))
X_A = permutation(lambda x, y, z, c: (x ^ near(c), y, z, c))
X_B = permutation(lambda x, y, z, c: (x ^ far(c), y, z, c))
SLOTS = [
    permutation(lambda x, y, z, c: (x, y, z, 1 - c)),
    permutation(lambda x, y, z, c: (x, y, z ^ near(c), c)),
    permutation(lambda x, y, z, c: (x, y, z ^ far(c), 1 - c)),
    permutation(lambda x, y, z, c: (x, y, z ^ far(c), c)),
    permutation(lambda x, y, z, c: (x, y, z ^ near(c), 1 - c)),
    permutation(lambda x, y, z, c: (x, y, z ^ 2, c)),
    permutation(lambda x, y, z, c: (x, y, z ^ 2, 1 - c)),
]
HALVES = permutation(lambda x, y, z, c: (x, y, z ^ 1, c))


LANES = (
    ("y1b", "y1f", "y2a"),
    ("y1a", "y2b", "y2f"),
    ("Bza", "Bzb", "Az2", "Bz2"),
    ("Bzbc", "Bzac", "Az2c", "Bz2c"),
    ("xPb", "xPf", "xQa", "xSb", "xSf"),
    ("xPa", "xQb", "xQf", "xSa"),
)
SLOT_NAMES = ("cc", "za", "zbc", "zb", "zac", "z2", "z2c")


def send(value, pairs):
    return lax.ppermute(value, AXES, pairs)


def after(value, *others):
    return lax.optimization_barrier((value,) + others)[0] if others else value


def basis_table(bins):
    lag = jnp.arange(SAMPLES, dtype=jnp.int32)
    taper = 0.5 - 0.5 * jnp.cos(2.0 * math.pi * (lag.astype(F32) + 0.5) / WINDOW)
    clipped = jnp.clip(lag, 0, WINDOW - 1)
    phase = bins[:, None] * clipped[None, :] % NFFT
    angle = 2.0 * math.pi * phase.astype(F32) / NFFT
    weight = jnp.where(lag < WINDOW, taper, 0.0)[None, :]
    both = jnp.stack([weight * jnp.cos(angle), -weight * jnp.sin(angle)], axis=1)
    return both.astype(BF16).reshape(16, SAMPLES)


def lag_rows(offsets):
    tick = jnp.arange(SAMPLES, dtype=jnp.int32)
    lag = tick[None, :, None] - offsets.reshape(-1, 1, SUB)
    return lag.reshape(-1, 1, SAMPLES * SUB)


def spectra_kernel(halves, place, table, lags, traces, *refs):
    outs, weights, result, masks = refs[:8], refs[8], refs[9], refs[10]
    step = pl.program_id(0)
    stations = lags.shape[0] * SUB
    lanes = SAMPLES * SUB

    @pl.when(step == 0)
    def _():
        lane = lax.broadcasted_iota(jnp.int32, (16, 128), 1) % SUB
        for n in range(SUB):
            masks[n] = jnp.where(lane == n, 1.0, 0.0).astype(BF16)

    def build(group):
        tick = lax.broadcasted_iota(jnp.int32, (SAMPLES, lanes), 0)
        for sub in range(GROUP // SUB):
            lag = lags[pl.ds(step * (STEP // SUB) + group * (GROUP // SUB) + sub, 1)].reshape(1, lanes)
            onehot = jnp.where(tick == lag, 1.0, 0.0).astype(BF16)
            basis = jnp.dot(table[...], onehot, preferred_element_type=F32).astype(BF16)
            for n in range(SUB):
                mask = masks[n]
                for at in range(0, lanes, 128):
                    weights[group, sub, pl.ds(n * 16, 16), pl.ds(at, 128)] = basis[:, at:at + 128] * mask

    def multiply(group):
        block = traces[:, pl.ds(group * GROUP, GROUP), :].astype(F32)
        for sub in range(GROUP // SUB):
            part = block[:, sub * SUB:(sub + 1) * SUB, :].reshape(lanes, halves * 128).astype(BF16)
            spectrum = jnp.dot(weights[group, sub], part, preferred_element_type=F32)
            for half in range(halves):
                result[group, half, pl.ds(sub * 128, 128), :] = spectrum[:, half * 128:half * 128 + 128]

    def store(group):
        first = step * STEP + group * GROUP
        for slot in range(8):
            for part in range(2):
                picked = pl.ds(slot * 2 + part, GROUP, 16)
                for half in range(halves):
                    base = (half ^ place[0]) * 2 * stations if halves == 2 else 0
                    at = pl.multiple_of(base + part * stations + first, GROUP)
                    outs[slot][pl.ds(at, GROUP), :] = result[group, half, picked, :].astype(BF16)

    groups = STEP // GROUP
    build(0)
    for group in range(groups):
        if group + 1 < groups:
            build(group + 1)
        multiply(group)
        if group:
            store(group - 1)
    store(groups - 1)


def spectra(place, table, lags, traces):
    stations, width = traces.shape[1:]
    rows = 2 * stations * (width // 128)
    whole = lambda *shape: pl.BlockSpec(shape, lambda s, _: (0,) * len(shape))
    return pl.pallas_call(
        functools.partial(spectra_kernel, width // 128),
        grid_spec=pltpu.PrefetchScalarGridSpec(
            num_scalar_prefetch=1,
            grid=(stations // STEP,),
            in_specs=[
                whole(16, SAMPLES),
                whole(*lags.shape),
                pl.BlockSpec((SAMPLES, STEP, width), lambda s, _: (0, s, 0)),
            ],
            out_specs=[whole(rows, 128)] * 8,
            scratch_shapes=[
                pltpu.VMEM((STEP // GROUP, GROUP // SUB, SUB * 16, SAMPLES * SUB), BF16),
                pltpu.VMEM((STEP // GROUP, width // 128, 256, 128), F32),
                pltpu.VMEM((SUB, 16, 128), BF16),
            ],
        ),
        out_shape=[jax.ShapeDtypeStruct((rows, 128), BF16)] * 8,
        compiler_params=pltpu.CompilerParams(vmem_limit_bytes=(48 if width == 128 else 28) << 20),
        cost_estimate=pl.CostEstimate(flops=8 << 30, bytes_accessed=10 << 20, transcendentals=0),
        name="spectra",
    )(place, table, lags, traces)


def correlate_kernel(pairs, picks, parts, part_out, has_start, place, *refs):
    a_in, b_in, refs = refs[:4], refs[4:8], refs[8:]
    start, refs = (refs[0], refs[1:]) if has_start else (None, refs)
    out, a_all, b_all, total, a_sems, b_sems = refs
    core = place[1]
    entry = 0 if picks is None else 2 * jnp.where(core == 0, picks[0], picks[1])

    a_copies = [pltpu.make_async_copy(a_in[n], a_all.at[n], a_sems.at[n]) for n in range(4)]
    b_copies = [
        pltpu.make_async_copy(b_in[n].at[pl.ds(entry, 2)], b_all.at[place[6 + n]], b_sems.at[n])
        for n in range(4)
    ]
    for copy in b_copies + a_copies:
        copy.start()
    for copy in b_copies:
        copy.wait()

    scale = 1.0 / K_AUX
    for n in range(4):
        a_copies[n].wait()
        q = place[2 + n]
        for at, part in enumerate(parts):
            right = []
            for z, half in pairs:
                for other in range(2):
                    for p in range(2):
                        piece = b_all[q, other, half, p ^ part]
                        right.append(-piece if part == 1 and p == 0 else piece)
            right = jnp.concatenate(right, axis=1)
            for block in range(2):
                rows = pl.ds(block * 256, 256)
                left = [
                    a_all[n, 2 * z + other, p, rows, :]
                    for z, _ in pairs
                    for other in range(2)
                    for p in range(2)
                ]
                term = lax.dot_general(
                    jnp.concatenate(left, axis=1),
                    right,
                    (((1,), (1,)), ((), ())),
                    preferred_element_type=F32,
                )
                if n > 0:
                    term += total[at, rows, :]
                elif has_start:
                    term += start[at, rows, :]
                if n < 3:
                    total[at, rows, :] = term
                elif part_out == "sum":
                    out[at, rows, :] = term
                elif part_out == "send":
                    out[at, rows, :] = (term * scale).astype(BF16)
                else:
                    out[0, at, rows, :] = term * scale


def correlate(place, a_pieces, b_pieces, pairs, picks, part_out, start=None, parts=(0, 1)):
    whole = lambda *shape: pl.BlockSpec(shape, lambda s, _: (0,) * len(shape))
    out, out_spec = jax.ShapeDtypeStruct((2, 512, 256), F32), whole(2, 512, 256)
    if part_out == "send":
        out, out_spec = jax.ShapeDtypeStruct((len(parts), 512, 256), BF16), whole(len(parts), 512, 256)
    elif part_out == "keep":
        out = jax.ShapeDtypeStruct((2, 2, 512, 256), F32)
        out_spec = pl.BlockSpec((1, 2, 512, 256), lambda s, place: (place[0], 0, 0, 0))
    starts = [] if start is None else [start]
    return pl.pallas_call(
        functools.partial(correlate_kernel, pairs, picks, parts, part_out, start is not None),
        grid_spec=pltpu.PrefetchScalarGridSpec(
            num_scalar_prefetch=1,
            grid=(1,),
            in_specs=[pl.BlockSpec(memory_space=pl.ANY)] * 8
            + [pl.BlockSpec((len(parts), 512, 256), lambda s, _: (parts[0] // len(parts), 0, 0))] * len(starts),
            out_specs=out_spec,
            scratch_shapes=[
                pltpu.VMEM((4, 4, 2, 512, 128), BF16),
                pltpu.VMEM((4, 2, 2, 2, 256, 128), BF16),
                pltpu.VMEM((2, 512, 256), F32),
                pltpu.SemaphoreType.DMA((4,)),
                pltpu.SemaphoreType.DMA((4,)),
            ],
        ),
        out_shape=out,
        compiler_params=pltpu.CompilerParams(vmem_limit_bytes=20 << 20),
        cost_estimate=pl.CostEstimate(
            flops=(32 if part_out == "send" else 2) << 30, bytes_accessed=6 << 20, transcendentals=0
        ),
        name="correlate",
    )(place, *a_pieces, *b_pieces, *starts)


KEEP = ((0, 0), (1, 1))
SEND = ((0, 1), (1, 0))


def finish_kernel(to, got, whole, out, narrow, wide, in_sems, out_sems):
    del whole
    slot = 1 - lax.axis_index("col") % 2
    blocks = [(part, pl.ds(half * 256, 256)) for part in range(got.shape[0]) for half in range(2)]
    ins = [
        pltpu.make_async_copy(got.at[part, rows], narrow.at[part, rows], in_sems.at[n])
        for n, (part, rows) in enumerate(blocks)
    ]
    outs = [
        pltpu.make_async_copy(wide.at[part, rows], out.at[slot, to + part, rows], out_sems.at[n])
        for n, (part, rows) in enumerate(blocks)
    ]
    for copy in ins:
        copy.start()
    for n, (part, rows) in enumerate(blocks):
        ins[n].wait()
        wide[part, rows, :] = narrow[part, rows, :].astype(F32)
        outs[n].start()
    for copy in outs:
        copy.wait()


def finish(got, whole, part):
    return pl.pallas_call(
        functools.partial(finish_kernel, part),
        in_specs=[pl.BlockSpec(memory_space=pl.ANY)] * 2,
        out_specs=pl.BlockSpec(memory_space=pl.ANY),
        scratch_shapes=[
            pltpu.VMEM(got.shape, BF16),
            pltpu.VMEM(got.shape, F32),
            pltpu.SemaphoreType.DMA((2,)),
            pltpu.SemaphoreType.DMA((2,)),
        ],
        out_shape=jax.ShapeDtypeStruct((2, 2, 512, 256), F32),
        input_output_aliases={1: 0},
        compiler_params=pltpu.CompilerParams(vmem_limit_bytes=8 << 20),
        name="finish",
    )(got, whole)


def local(traces_rows, traces_cols, offsets_rows, offsets_cols, bins):
    layer, x, col = (lax.axis_index(axis) for axis in AXES)
    y, zl, zh, core = col // 2, col % 2, layer // 2, layer % 2
    z = 2 * zh + zl
    one, three = 1 + 2 * core, 3 - 2 * core
    place = jnp.stack(
        [zl, core, y, y ^ one, y ^ three, y ^ 2, x, x ^ one, x ^ three, x ^ 2]
    ).astype(jnp.int32)

    dests = [
        (z, core), (z, 1 - core), (z ^ one, core), (z ^ three, 1 - core),
        (z ^ three, core), (z ^ one, 1 - core), (z ^ 2, core), (z ^ 2, 1 - core),
    ]
    order = jnp.stack([4 * (a // 2) + 2 * b + a % 2 for a, b in dests])
    picked = jnp.sum(jnp.where(order[:, None] == jnp.arange(8)[None, :], bins[None, :], 0), axis=1)
    table = basis_table(picked)
    a_own, *a_away = spectra(place, table, lag_rows(offsets_rows), traces_rows)
    b_own, *b_away = spectra(after(place, a_own), table, lag_rows(offsets_cols), traces_cols)

    slabs = {"A" + name: slab for name, slab in zip(SLOT_NAMES, a_away)}
    slabs.update({"B" + name: slab for name, slab in zip(SLOT_NAMES, b_away)})
    moves = {array + name: pairs for name, pairs in zip(SLOT_NAMES, SLOTS) for array in "AB"}
    moves.update(ya=Y_A, yb=Y_B, yf=Y_A, xa=X_A, xb=X_B, xf=X_A)
    before = {name: lane[n - 1] for lane in LANES for n, name in enumerate(lane) if n}
    got, chunks = {}, {}

    def build(name):
        axis, which = name
        array, own = ("A", a_own) if axis == "y" else ("B", b_own)
        slots = lambda *names: jnp.stack([arrival(array + n) for n in names])
        if axis == "y":
            q, r = slots("za", "zbc"), slots("zb", "zac")
            if which == "1":
                parts = [own[None], slots("cc"), jnp.where(core == 0, q, r)]
            else:
                parts = [slots("z2", "z2c"), jnp.where(core == 0, r, q)]
            return jnp.concatenate(parts).reshape(4, 2, 512, 128)
        if which == "P":
            parts = [own[None], slots("cc")]
        elif which == "Q":
            parts = [slots("za", "zbc", "zb", "zac")]
        else:
            parts = [slots("z2", "z2c")]
        return jnp.concatenate(parts).reshape(-1, 2, 2, 256, 128)

    def chunk(name):
        if name not in chunks:
            chunks[name] = build(name)
        return chunks[name]

    def arrival(name):
        if name not in got:
            if name in slabs:
                value, move = slabs[name], moves[name]
            else:
                which, way = name[:2], name[2]
                value = arrival(which + "b") if way == "f" else chunk(which)
                move = moves[name[0] + way]
            if name in before:
                value = after(value, arrival(before[name]))
            with jax.named_scope("send_" + name):
                got[name] = send(value, move)
        return got[name]

    pieces = {
        name: [chunk(name)] + [arrival(name + way) for way in "abf"] for name in ("y1", "y2", "xP", "xQ", "xS")
    }
    keep_early = correlate(place, pieces["y1"], pieces["xP"], KEEP, None, "sum")
    send_early = correlate(place, pieces["y1"], pieces["xQ"], SEND, (0, 1), "sum")
    arrived, wait = [], (keep_early,)
    for part in range(2):
        leaves = correlate(
            after(place, *wait), pieces["y2"], pieces["xQ"], SEND, (1, 0), "send", send_early, (part,)
        )
        arrived.append(send(leaves, HALVES))
        wait = (leaves,)
    stays = correlate(after(place, leaves), pieces["y2"], pieces["xS"], KEEP, None, "keep", keep_early)
    for part, half in enumerate(arrived):
        stays = finish(half, stays, part)
    return stays


def solution(mesh):
    return jax.shard_map(
        local,
        mesh=mesh,
        in_specs=(
            P(None, "row", ("layer", "col")),
            P(None, "col", ("layer", "row")),
            P("row"),
            P("col"),
            P(),
        ),
        out_specs=P("layer", None, "row", "col"),
        check_vma=False,
    )
```
